512 devices in a mesh: gx: 64 (over x_hi, z, core), gy: 8 (over x_lo, y).
Axes of the slice: x: 4 (x_hi: 2, x_lo: 2; x = x_hi * 2 + x_lo), y: 4, z: 16, core: 2. Of those that a mesh axis runs over, the one named last changes fastest.
Arguments:
- velocity: float32 [3, 16, 1024, 1024], P(None, None, 'gx', 'gy'), may hold values from -4 to 4
- theta_field: float32 [16, 1024, 1024], P(None, 'gx', 'gy'), may hold values from -5 to 5
- vapour: float32 [16, 1024, 1024], P(None, 'gx', 'gy'), may hold values from 8 to 11
- radius: float32 [5, 16, 1024, 1024], P(None, None, 'gx', 'gy'), may hold values from 1 to 10
- multiplicity: float32 [5, 16, 1024, 1024], P(None, None, 'gx', 'gy'), may hold values from 0.5 to 5
- solute: float32 [5, 16, 1024, 1024], P(None, None, 'gx', 'gy'), may hold values from 0.1 to 1
- counts: int32 [16, 1024, 1024], P(None, 'gx', 'gy'), may hold values from 3 to 5, as said below
- leave_slot: int32 [64, 8, 8192], P('gx', 'gy'), may hold values from -1 to 163839, as said below
- leave_dir: int32 [64, 8, 8192], P('gx', 'gy'), may hold values from 0 to 3, as said below
Outputs:
- state_new: float32 [5, 16, 1024, 1024], P(None, None, 'gx', 'gy')
- radius_new: float32 [5, 16, 1024, 1024], P(None, None, 'gx', 'gy')
- arrivals: float32 [3, 4, 64, 8, 2048], P(None, None, 'gx', 'gy')
The draws below stay inside these ranges and needn't reach their ends.
Inputs may be any that keep to these rules, and one draw needn't show every extreme that they name: Slots 0 to counts - 1 of a cell hold live droplets; the others are unused. `leave_slot`: -1 marks an empty entry; the other entries of a tile are distinct indices of live droplets of that tile, in the local index of the steps. A tile's list sends at most 2048 droplets in one direction, and some tile sends exactly 2048 in some direction. `leave_dir`: 0: +x, 1: -x, 2: +y, 3: -y; meaningless where leave_slot is -1.
All inputs are finite; a program needn't handle non-finite values.
Results may differ from the reference program's by a relative error of at most 0.0003.
Values sent between devices are 32-bit elements; how exact they have to be, the bound alone decides.
A program may use at most 64 MiB of HBM per device.

```python
import math
import jax
import jax.numpy as jnp
from jax import lax

CX = 16
CY = 128
NZ = 16
SLOTS = 5
CAP = 2048
MIG = 8192
TILES_X = 64
TILES_Y = 8
NX = 1024
NY = 1024


def migration_lists(key):
    cell_count = NZ * CX * CY
    tile_count = TILES_X * TILES_Y
    counts = jax.random.randint(jax.random.fold_in(key, 101), (NZ, NX, NY), 3, SLOTS + 1)
    local_counts = counts.reshape(NZ, TILES_X, CX, TILES_Y, CY).transpose(1, 3, 0, 2, 4).reshape(tile_count, cell_count)
    extra_draw = jax.random.randint(jax.random.fold_in(key, 102), (tile_count, 4), 0, CAP // 2 + 1)
    per_way = CAP // 2 + extra_draw
    forced = jax.random.randint(jax.random.fold_in(key, 104), (), 0, tile_count * 4)
    per_way = jnp.where(jnp.arange(tile_count * 4).reshape(tile_count, 4) == forced, CAP, per_way)
    cumulative = jnp.cumsum(per_way, axis=1)
    places = jnp.arange(MIG)
    sorted_way = jnp.sum((places[None, :, None] >= cumulative[:, None, :3]).astype(jnp.int32), axis=2)
    listed_sorted = places[None] < cumulative[:, 3:4]
    orders = jax.vmap(lambda subkey: jax.random.permutation(subkey, MIG))(jax.random.split(jax.random.fold_in(key, 105), tile_count))
    ways = jnp.take_along_axis(sorted_way, orders, 1)
    listed = jnp.take_along_axis(listed_sorted, orders, 1)
    offset = jax.random.randint(jax.random.fold_in(key, 106), (tile_count, 1), 0, cell_count)
    stride = 2 * jax.random.randint(jax.random.fold_in(key, 107), (tile_count, 1), 0, cell_count // 2) + 1
    cell_index = (offset + places[None] * stride) % cell_count
    limits = jnp.take_along_axis(local_counts, cell_index, 1)
    in_cell = jax.random.randint(jax.random.fold_in(key, 108), (tile_count, MIG), 0, limits)
    flat_index = in_cell * cell_count + cell_index
    leave_slot = jnp.where(listed, flat_index, -1).reshape(TILES_X, TILES_Y, MIG)
    leave_dir = ways.reshape(TILES_X, TILES_Y, MIG)
    return (counts, leave_slot, leave_dir)


def draw_counts(key, part):
    shared = migration_lists(key)
    return shared[0].astype(jnp.int32)


def draw_leave_slot(key, part):
    shared = migration_lists(key)
    return shared[1].astype(jnp.int32)


def draw_leave_dir(key, part):
    shared = migration_lists(key)
    return shared[2].astype(jnp.int32)


def steps_of(stream_key, shape, cuts, smallest, top_value):
    level, own = 1.0, jax.random.fold_in(stream_key, 6)
    for position, parts in cuts:
        heights = jnp.exp(jax.random.uniform(jax.random.fold_in(own, position), (parts,), jnp.float32, smallest / len(cuts), top_value / len(cuts)))
        level = level * jnp.repeat(heights, shape[position] // parts).reshape([-1 if axis == position else 1 for axis in range(len(shape))])
    return level


def gaussian(rng, extent, deviation, limit, pieces=(), held_as=jnp.bfloat16):
    values = deviation * jax.random.normal(rng, extent, jnp.float32)
    if pieces:
        values = values * steps_of(rng, extent, pieces, -0.22, 0.18)
    return jnp.clip(values, -limit, limit).astype(held_as)


def setup_inputs(seed: int = 0) -> dict:
    key_list = jax.random.split(jax.random.key(seed), 10)
    velocity = gaussian(key_list[0], (3, NZ, NX, NY), 1.0, 4.0, ((2, 64), (3, 8)), jnp.float32)
    theta_field = gaussian(key_list[1], (NZ, NX, NY), 1.0, 5.0, ((1, 64), (2, 8)), jnp.float32)
    vapour = jnp.clip(8.0 + 3.0 * jax.random.uniform(key_list[2], (NZ, NX, NY), jnp.float32) ** steps_of(key_list[2], (NZ, NX, NY), ((1, 64), (2, 8)), -0.2, 0.2), 8.0, 11.0)
    radius = jnp.clip(jnp.exp(math.log(10.0) - 2.3025851 * jax.random.uniform(key_list[3], (SLOTS, NZ, NX, NY), jnp.float32) ** steps_of(key_list[3], (SLOTS, NZ, NX, NY), ((2, 64), (3, 8)), -0.2, 0.2)), 1.0, 10.0)
    multiplicity = jnp.clip(jnp.exp(math.log(5.0) - 2.3025851 * jax.random.uniform(key_list[4], (SLOTS, NZ, NX, NY), jnp.float32) ** steps_of(key_list[4], (SLOTS, NZ, NX, NY), ((2, 64), (3, 8)), -0.2, 0.2)), 0.5, 5.0)
    solute = jnp.clip(jnp.exp(math.log(1.0) - 2.3025851 * jax.random.uniform(key_list[5], (SLOTS, NZ, NX, NY), jnp.float32) ** steps_of(key_list[5], (SLOTS, NZ, NX, NY), ((2, 64), (3, 8)), -0.2, 0.2)), 0.1, 1.0)
    counts = draw_counts(jax.random.fold_in(key_list[9], 71), 0)
    leave_slot = draw_leave_slot(jax.random.fold_in(key_list[9], 71), 0)
    leave_dir = draw_leave_dir(jax.random.fold_in(key_list[9], 71), 0)
    return dict(velocity=velocity, theta_field=theta_field, vapour=vapour, radius=radius, multiplicity=multiplicity, solute=solute, counts=counts, leave_slot=leave_slot, leave_dir=leave_dir)


TIME_STEP = 0.5
DIFFUSION = 0.05
BUOYANCY = 0.0327
SATURATION = 10.0
SAT_SLOPE = 0.06
GROWTH = 20.0
CURVATURE = 1.0
HYGROSCOPY = 1.0
FLOOR_SQUARE = 0.25
UPTAKE = 0.001
HEATING = 2.5

def advance(padded, velocity, theta_field):
    span_x = padded.shape[2] - 6
    span_y = padded.shape[3] - 6

    def along_x(offset):
        return padded[:, :, 3 + offset:3 + offset + span_x, 3:3 + span_y]

    def along_y(offset):
        return padded[:, :, 3:3 + span_x, 3 + offset:3 + offset + span_y]

    def centred(select):
        return (select(3) - 9.0 * select(2) + 45.0 * select(1) - 45.0 * select(-1) + 9.0 * select(-2) - select(-3)) / 60.0

    def damping(select):
        return (select(3) - 6.0 * select(2) + 15.0 * select(1) - 20.0 * select(0) + 15.0 * select(-1) - 6.0 * select(-2) + select(-3)) / 60.0
    middle = along_x(0)
    east_wind = velocity[0][None]
    north_wind = velocity[1][None]
    rising = velocity[2][None]
    upper_cells = jnp.concatenate([middle[:, 1:], middle[:, -1:]], 1)
    lower_cells = jnp.concatenate([middle[:, :1], middle[:, :-1]], 1)
    transport = east_wind * centred(along_x) - jnp.abs(east_wind) * damping(along_x)
    transport = transport + north_wind * centred(along_y) - jnp.abs(north_wind) * damping(along_y)
    transport = transport + rising * (upper_cells - lower_cells) * 0.5
    mixing = DIFFUSION * (along_x(1) + along_x(-1) + along_y(1) + along_y(-1) + upper_cells + lower_cells - 6.0 * middle)
    result = middle + TIME_STEP * (mixing - transport)
    buoyant = jnp.zeros_like(result).at[2].set(TIME_STEP * BUOYANCY * theta_field)
    return result + buoyant

def saturation(theta_new, vapour_new):
    return vapour_new / (SATURATION * jnp.exp(SAT_SLOPE * theta_new)) - 1.0

def grow_radius(radius, solute, supersat):
    square = radius * radius + GROWTH * (supersat - CURVATURE / radius + HYGROSCOPY * solute / (radius * radius * radius))
    return jnp.sqrt(jnp.maximum(square, FLOOR_SQUARE))

def compact(values, selected):
    rank_list = jnp.cumsum(selected.astype(jnp.int32)) - 1
    target = jnp.where(selected, rank_list, CAP)
    return jnp.zeros((values.shape[0], CAP), values.dtype).at[:, target].set(values, mode='drop')

def reference(velocity, theta_field, vapour, radius, multiplicity, solute, counts, leave_slot, leave_dir):
    fields = jnp.concatenate([velocity, theta_field[None], vapour[None]], 0)
    padded = jnp.pad(fields, ((0, 0), (0, 0), (3, 3), (3, 3)), mode='wrap')
    advanced = advance(padded, velocity, theta_field)
    supersat = saturation(advanced[3], advanced[4])
    grown = lax.map(lambda couple: grow_radius(couple[0], couple[1], supersat), (radius, solute))
    alive_mask = jnp.arange(SLOTS)[:, None, None, None] < counts[None]
    condensed = lax.optimization_barrier(jnp.sum(jnp.where(alive_mask, multiplicity * (grown * grown * grown - radius * radius * radius), 0.0), 0))
    theta_new = advanced[3] + HEATING * UPTAKE * condensed
    vapour_new = advanced[4] - UPTAKE * condensed
    state_new = jnp.concatenate([advanced[:3], theta_new[None], vapour_new[None]], 0)
    slot_total = SLOTS * NZ * CX * CY

    def to_tiles(array):
        return array.reshape(SLOTS, NZ, TILES_X, CX, TILES_Y, CY).transpose(2, 4, 0, 1, 3, 5).reshape(TILES_X, TILES_Y, slot_total)

    def from_tiles(array):
        return array.reshape(TILES_X, TILES_Y, SLOTS, NZ, CX, CY).transpose(2, 3, 0, 4, 1, 5).reshape(SLOTS, NZ, NX, NY)
    is_listed = leave_slot >= 0
    departed_tiles = jax.vmap(jax.vmap(lambda slot_index: jnp.zeros(slot_total + 1, jnp.bool_).at[slot_index].set(True)))(jnp.where(is_listed, leave_slot, slot_total))
    departed = from_tiles(departed_tiles[:, :, :slot_total])
    radius_new = jnp.where(alive_mask & jnp.logical_not(departed), grown, 0.0)
    safe_index = jnp.where(is_listed, leave_slot, 0)
    picked = jnp.stack([jnp.take_along_axis(to_tiles(source), safe_index, 2) for source in (grown, multiplicity, solute)], 2)

    def buckets(values, chosen, heading):
        return jnp.stack([compact(values, chosen & (heading == number)) for number in range(4)], 1)
    bucketed = jax.vmap(jax.vmap(buckets))(picked, is_listed, leave_dir)
    ordered = jnp.transpose(bucketed, (2, 3, 0, 1, 4))
    arrivals = jnp.stack([jnp.roll(ordered[:, 0], 1, 1), jnp.roll(ordered[:, 1], -1, 1), jnp.roll(ordered[:, 2], 1, 2), jnp.roll(ordered[:, 3], -1, 2)], 1)
    return (state_new, radius_new, arrivals)
```

```python
import functools

import jax
import jax.numpy as jnp
from jax import lax
from jax.experimental import pallas as pl
from jax.experimental.pallas import tpu as pltpu
from jax.sharding import PartitionSpec as P

MESH = pl.DeviceIdType.MESH
VMEM_SPEC = pl.BlockSpec(memory_space=pltpu.VMEM)
ANY_SPEC = pl.BlockSpec(memory_space=pl.ANY)

CX, CY, NZ, SLOTS, CAP, MIG = 16, 128, 16, 5, 2048, 8192
TILES = SLOTS * NZ * 2
BLOCKS = MIG // 128
BINS = 64
PH = 4 * CAP // 128
GROUP = 6

TIME_STEP = 0.5
DIFFUSION = 0.05
BUOYANCY = 0.0327
SATURATION = 10.0
SAT_SLOPE = 0.06
GROWTH = 20.0
CURVATURE = 1.0
HYGROSCOPY = 1.0
FLOOR_SQUARE = 0.25
UPTAKE = 0.001
HEATING = 2.5

F32, BF16, I32 = jnp.float32, jnp.bfloat16, jnp.int32


def iota(shape, dim):
    return lax.broadcasted_iota(I32, shape, dim)


def ring(axis):
    count = lax.axis_size(axis)
    me = lax.axis_index(axis)
    return {axis: lax.rem(me + 1, count)}, {axis: lax.rem(me + count - 1, count)}


def greet(neighbours):
    barrier = pltpu.get_barrier_semaphore()
    for there in neighbours:
        pl.semaphore_signal(barrier, inc=1, device_id=there, device_id_type=MESH)
    pl.semaphore_wait(barrier, len(neighbours))


def halo_kernel(vel, theta, vap, pad, yhalo, fields, packed, landed, local_sem, send_sem, recv_sem):
    east, west = ring("gx")
    north, south = ring("gy")
    parts = ((vel, 0, 3), (theta, 3, 1), (vap, 4, 1))

    def part(ref, rows):
        return ref.at[:, :, rows, :] if len(ref.shape) == 4 else ref.at[:, rows, :]

    def place(ref, first, count, rows):
        if count > 1:
            return ref.at[first : first + count, :, rows, :]
        return ref.at[first, :, rows, :]

    loads = [
        pltpu.make_async_copy(ref, place(fields, first, count, slice(None)), local_sem.at[number])
        for number, (ref, first, count) in enumerate(parts)
    ]
    for copy in loads:
        copy.start()
    greet((east, west, north, south))
    sends = []
    for number, (ref, first, count) in enumerate(parts):
        for way, (there, rows, target) in enumerate(
            ((east, slice(13, 16), slice(5, 8)), (west, slice(0, 3), slice(24, 27)))
        ):
            sends.append(
                pltpu.make_async_remote_copy(
                    src_ref=part(ref, rows),
                    dst_ref=place(pad, first, count, target),
                    send_sem=send_sem.at[number * 2 + way],
                    recv_sem=recv_sem.at[number * 2 + way],
                    device_id=there,
                    device_id_type=MESH,
                )
            )
            sends[-1].start()
    for copy in loads:
        copy.wait()
    inner = pltpu.make_async_copy(fields, pad.at[:, :, 8:24, :], local_sem.at[3])
    inner.start()

    lane = iota((16, 128), 1)
    turned = lax.rem(lane + 3, 128)
    number = turned // GROUP

    def pack(quarter, _):
        total = jnp.zeros((16, 128), F32)
        for inner_level in range(4):
            for f in range(5):
                g = inner_level * 5 + f
                value = fields[f, quarter * 4 + inner_level]
                if g:
                    value = pltpu.roll(value, GROUP * g, 1)
                total = jnp.where(number == g, value, total)
        packed[quarter] = total
        return _

    lax.fori_loop(0, 4, pack, 0)
    for way, there in enumerate((north, south)):
        sends.append(
            pltpu.make_async_remote_copy(
                src_ref=packed,
                dst_ref=landed.at[way],
                send_sem=send_sem.at[6 + way],
                recv_sem=recv_sem.at[6 + way],
                device_id=there,
                device_id_type=MESH,
            )
        )
        sends[-1].start()
    sends[6].wait_recv()
    sends[7].wait_recv()
    from_south = turned - number * GROUP < 3
    for quarter in range(4):
        yhalo[quarter] = jnp.where(from_south, landed[0, quarter], landed[1, quarter])
    for copy in sends[:6]:
        copy.wait_recv()
    for copy in sends:
        copy.wait_send()
    inner.wait()


def exchange_halo(velocity, theta_field, vapour):
    return pl.pallas_call(
        halo_kernel,
        out_shape=(
            jax.ShapeDtypeStruct((5, NZ, 32, CY), F32),
            jax.ShapeDtypeStruct((4, 16, 128), F32),
        ),
        in_specs=[ANY_SPEC] * 3,
        out_specs=(ANY_SPEC, VMEM_SPEC),
        scratch_shapes=[
            pltpu.VMEM((5, NZ, CX, CY), F32),
            pltpu.VMEM((4, 16, 128), F32),
            pltpu.VMEM((2, 4, 16, 128), F32),
            pltpu.SemaphoreType.DMA((4,)),
            pltpu.SemaphoreType.DMA((8,)),
            pltpu.SemaphoreType.DMA((8,)),
        ],
        compiler_params=pltpu.CompilerParams(
            collective_id=0, has_side_effects=True, vmem_limit_bytes=16 << 20
        ),
    )(velocity, theta_field, vapour)


def physics(pad, yhalo, radius, mult, sol, counts, state, rnew, grown):
    lane = iota((8, 128), 1)

    def quarter_turn(quarter, _):
        for inner_level in range(4):
            k = quarter * 4 + inner_level
            above = jnp.minimum(k + 1, NZ - 1)
            below = jnp.maximum(k - 1, 0)
            for half in range(2):
                base = 8 + 8 * half
                rows = slice(8 * half, 8 * half + 8)
                u = pad[0, k, base : base + 8] * (-TIME_STEP / 60.0)
                v = pad[1, k, base : base + 8] * (-TIME_STEP / 60.0)
                w = pad[2, k, base : base + 8]
                lift = DIFFUSION * TIME_STEP - w * (0.5 * TIME_STEP)
                sink = DIFFUSION * TIME_STEP + w * (0.5 * TIME_STEP)
                u_size, v_size = jnp.abs(u), jnp.abs(v)
                halo_row = yhalo[quarter, rows]
                moved = []
                for f in range(5):
                    mid = pad[f, k, base : base + 8]

                    def x_at(d):
                        return pad[f, k, base + d : base + d + 8]

                    g = inner_level * 5 + f
                    edge = pltpu.roll(halo_row, 128 - GROUP * g, 1) if g else halo_row

                    def y_at(d):
                        if d > 0:
                            return pltpu.roll(jnp.where(lane < d, edge, mid), 128 - d, 1)
                        return pltpu.roll(jnp.where(lane >= 128 + d, edge, mid), -d, 1)

                    around = 0.0
                    total = mid
                    for at, wind, size in ((x_at, u, u_size), (y_at, v, v_size)):
                        p1, m1, p2, m2, p3, m3 = at(1), at(-1), at(2), at(-2), at(3), at(-3)
                        s1 = p1 + m1
                        total = total + wind * (45.0 * (p1 - m1) - 9.0 * (p2 - m2) + (p3 - m3))
                        total = total + size * (15.0 * s1 - 6.0 * (p2 + m2) + (p3 + m3) - 20.0 * mid)
                        around = around + s1
                    up = pad[f, above, base : base + 8]
                    down = pad[f, below, base : base + 8]
                    total = total + (DIFFUSION * TIME_STEP) * (around - 6.0 * mid)
                    total = total + lift * up + sink * down
                    if f == 2:
                        total = total + (TIME_STEP * BUOYANCY) * pad[3, k, base : base + 8]
                    moved.append(total)
                supersat = moved[4] * (jnp.exp(-SAT_SLOPE * moved[3]) * (1.0 / SATURATION)) - 1.0
                alive_count = counts[k, rows]
                condensed = jnp.zeros((8, 128), F32)
                for s in range(SLOTS):
                    tile = (s * NZ + k) * 2 + half
                    r = radius[tile]
                    inv = 1.0 / r
                    r2 = r * r
                    square = r2 + GROWTH * (
                        supersat - CURVATURE * inv + (HYGROSCOPY * sol[tile]) * (inv * inv * inv)
                    )
                    square = jnp.maximum(square, FLOOR_SQUARE)
                    new = jnp.sqrt(square)
                    alive = s < alive_count
                    grown[tile] = new
                    rnew[tile] = jnp.where(alive, new, 0.0)
                    condensed = condensed + jnp.where(
                        alive, mult[tile] * (square * new - r2 * r), 0.0
                    )
                state[0, k, rows] = moved[0]
                state[1, k, rows] = moved[1]
                state[2, k, rows] = moved[2]
                state[3, k, rows] = moved[3] + (HEATING * UPTAKE) * condensed
                state[4, k, rows] = moved[4] - UPTAKE * condensed
        return _

    lax.fori_loop(0, 4, quarter_turn, 0)


def to_bf16(mask):
    return jnp.where(mask, 1.0, 0.0).astype(BF16)


NT = (((1,), (1,)), ((), ()))
NN = (((1,), (0,)), ((), ()))


def dot(a, b, dims=NN):
    return lax.dot_general(a, b, dims, preferred_element_type=F32)


def rank_list(slots, ways, lanes_hot, bin_of, codes):
    before = iota((128, 128), 0) < iota((128, 128), 1)
    counter = jnp.concatenate([to_bf16(before), jnp.ones((128, 128), BF16)], 1)

    slot = slots[...]
    valid = slot >= 0
    way = jnp.where(valid, ways[...], -1)
    marks = [jnp.where(way == d, 1.0, 0.0) for d in range(4)]
    inside = dot(jnp.concatenate(marks, 0).astype(BF16), counter)
    earlier = to_bf16(iota((BLOCKS, BLOCKS), 1) < iota((BLOCKS, BLOCKS), 0))
    rank = jnp.zeros((BLOCKS, 128), F32)
    for d in range(4):
        block = inside[d * BLOCKS : (d + 1) * BLOCKS]
        offset = dot(earlier, block[:, 128:].astype(BF16))
        rank = rank + marks[d] * (block[:, :128] + offset)
    place = way * CAP + rank.astype(I32)
    row = lax.shift_right_logical(slot, 7)
    place_row = lax.shift_right_logical(place, 7)
    codes[0] = jnp.where(valid, lax.shift_right_logical(row, 3) + 1, 0).astype(F32)
    codes[1] = (((row & 1) << 7) + (place & 127)).astype(F32)
    codes[2] = (lax.shift_right_logical(row & 7, 1) + (place_row << 2)).astype(F32)

    def turn(t, carry):
        slot8 = slots[pl.ds(pl.multiple_of(t * 8, 8), 8)]
        lane8 = jnp.where(slot8 >= 0, slot8 & 127, -1)
        found = []
        for q in range(8):
            hit = iota((128, 128), 0) == lane8[q : q + 1]
            hot = to_bf16(hit)
            lanes_hot[:, pl.ds(pl.multiple_of(t * 1024 + q * 128, 128), 128)] = hot
            counted = dot(hot, counter)
            number = jnp.sum(jnp.where(hit, counted[:, :128] + carry, 0.0), axis=0, keepdims=True)
            found.append(number)
            carry = carry + counted[:, 128:]
        bin_of[pl.ds(pl.multiple_of(t * 8, 8), 8)] = jnp.concatenate(found, 0).astype(I32)
        return carry

    carry = lax.fori_loop(0, BLOCKS // 8, turn, jnp.zeros((128, 128), F32))
    return jnp.max(carry).astype(I32)


def pick_turn(chunk, lanes_hot, bin_of, codes, spread, table, tbl_int, grown, mult, sol, rnew, values, rows_hot, out_acc):
    def spread_turn(t, _):
        tile = pl.ds(pl.multiple_of(t * 8, 8), 8)
        bins8 = bin_of[tile] - chunk * BINS
        code8 = [codes[n, tile] for n in range(3)]
        for q in range(8):
            hit = iota((BINS, 128), 0) == bins8[q : q + 1]
            for n in range(3):
                spread[n * BINS : (n + 1) * BINS, pl.ds(pl.multiple_of(t * 1024 + q * 128, 128), 128)] = (
                    jnp.where(hit, code8[n][q : q + 1], 0.0).astype(BF16)
                )
        return _

    lax.fori_loop(0, BLOCKS // 8, spread_turn, 0)
    table[...] = dot(spread[...], lanes_hot[...], NT)
    first = table[0:BINS].astype(I32)
    second = table[BINS : 2 * BINS].astype(I32)
    third = table[2 * BINS : 3 * BINS].astype(I32)
    group = first - 1
    inner = lax.shift_right_logical(second, 7) + ((third & 3) << 1)
    place_row = jnp.where(first > 0, lax.shift_right_logical(third, 2), -1)
    place_lane = second & 127
    tbl_int[0] = place_row
    tbl_int[1] = place_lane

    groups = [group[8 * m : 8 * m + 8] for m in range(BINS // 8)]
    inners = [inner[8 * m : 8 * m + 8] for m in range(BINS // 8)]
    bits = [jnp.left_shift(1, inners[m]) for m in range(BINS // 8)]
    sublane = iota((8, 128), 0)

    def gather_turn(j, kept):
        sources = (grown[j], mult[j], sol[j])
        kept = list(kept)
        marked = jnp.zeros((8, 128), I32)
        for m in range(BINS // 8):
            hit = groups[m] == j
            marked = marked | jnp.where(hit, bits[m], 0)
            for n in range(3):
                got = jnp.take_along_axis(sources[n], inners[m], axis=0, mode="promise_in_bounds")
                kept[n * (BINS // 8) + m] = jnp.where(hit, got, kept[n * (BINS // 8) + m])
        marked = marked | pltpu.roll(marked, 4, 0)
        marked = marked | pltpu.roll(marked, 2, 0)
        marked = marked | pltpu.roll(marked, 1, 0)
        left = lax.shift_right_logical(marked, sublane) & 1
        rnew[j] = jnp.where(left == 1, 0.0, rnew[j])
        return tuple(kept)

    kept = lax.fori_loop(
        0, TILES, gather_turn, tuple(jnp.zeros((8, 128), F32) for _ in range(3 * BINS // 8))
    )
    for n in range(3):
        for m in range(BINS // 8):
            values[n, 8 * m : 8 * m + 8] = kept[n * (BINS // 8) + m]

    def place_turn(t, _):
        tile = pl.ds(pl.multiple_of(t * 8, 8), 8)
        row8, lane8 = tbl_int[0, tile], tbl_int[1, tile]
        high = [values[n, tile].astype(BF16).astype(F32) for n in range(3)]
        low = [values[n, tile] - high[n] for n in range(3)]
        for q in range(8):
            columns = slice(q * 128, q * 128 + 128)
            hit = iota((PH, 128), 0) == row8[q : q + 1]
            for n, piece in enumerate(high + low):
                spread_out = jnp.where(hit, piece[q : q + 1], 0.0).astype(BF16)
                rows_hot[n * PH : (n + 1) * PH, columns] = spread_out
            rows_hot[6 * PH :, columns] = to_bf16(iota((128, 128), 0) == lane8[q : q + 1])
        out_acc[...] += dot(rows_hot[: 6 * PH], rows_hot[6 * PH :], NT)
        return _

    lax.fori_loop(0, BINS // 8, place_turn, 0)


def local_kernel(
    pad, yhalo, radius, mult, sol, counts, slots, ways,
    state, rnew, outgoing,
    grown, lanes_hot, bin_of, codes, spread, table, tbl_int, values, rows_hot, out_acc,
):
    physics(pad, yhalo, radius, mult, sol, counts, state, rnew, grown)
    most = rank_list(slots, ways, lanes_hot, bin_of, codes)
    out_acc[...] = jnp.zeros_like(out_acc)

    def turn(chunk, _):
        pick_turn(
            chunk, lanes_hot, bin_of, codes, spread, table, tbl_int,
            grown, mult, sol, rnew, values, rows_hot, out_acc,
        )
        return _

    lax.fori_loop(0, (most + BINS - 1) // BINS, turn, 0)
    for d in range(4):
        for n in range(3):
            first = n * PH + d * 16
            outgoing[d, n] = out_acc[first : first + 16] + out_acc[first + 3 * PH : first + 3 * PH + 16]


def local_step(pad, yhalo, radius, multiplicity, solute, counts, slots, ways):
    return pl.pallas_call(
        local_kernel,
        out_shape=(
            jax.ShapeDtypeStruct((5, NZ, CX, CY), F32),
            jax.ShapeDtypeStruct((TILES, 8, 128), F32),
            jax.ShapeDtypeStruct((4, 3, CAP // 128, 128), F32),
        ),
        in_specs=[VMEM_SPEC] * 8,
        out_specs=(VMEM_SPEC,) * 3,
        scratch_shapes=[
            pltpu.VMEM((TILES, 8, 128), F32),
            pltpu.VMEM((128, MIG), BF16),
            pltpu.VMEM((BLOCKS, 128), I32),
            pltpu.VMEM((3, BLOCKS, 128), F32),
            pltpu.VMEM((3 * BINS, MIG), BF16),
            pltpu.VMEM((3 * BINS, 128), F32),
            pltpu.VMEM((2, BINS, 128), I32),
            pltpu.VMEM((3, BINS, 128), F32),
            pltpu.VMEM((6 * PH + 128, 1024), BF16),
            pltpu.VMEM((6 * PH, 128), F32),
        ],
        compiler_params=pltpu.CompilerParams(vmem_limit_bytes=40 << 20),
    )(pad, yhalo, radius, multiplicity, solute, counts, slots, ways)


def droplet_kernel(outgoing, arrivals, send_sem, recv_sem):
    east, west = ring("gx")
    north, south = ring("gy")
    ways = (east, west, north, south)
    greet(ways)
    sends = [
        pltpu.make_async_remote_copy(
            src_ref=outgoing.at[d],
            dst_ref=arrivals.at[:, d],
            send_sem=send_sem.at[d],
            recv_sem=recv_sem.at[d],
            device_id=there,
            device_id_type=MESH,
        )
        for d, there in enumerate(ways)
    ]
    for copy in sends:
        copy.start()
    for copy in sends:
        copy.wait()


def exchange_droplets(outgoing):
    return pl.pallas_call(
        droplet_kernel,
        out_shape=jax.ShapeDtypeStruct((3, 4, CAP // 128, 128), F32),
        in_specs=[ANY_SPEC],
        out_specs=ANY_SPEC,
        scratch_shapes=[pltpu.SemaphoreType.DMA((4,)), pltpu.SemaphoreType.DMA((4,))],
        compiler_params=pltpu.CompilerParams(collective_id=1, has_side_effects=True),
    )(outgoing)


def per_device(
    velocity, theta_field, vapour, radius, multiplicity, solute, counts, leave_slot, leave_dir
):
    pad, yhalo = exchange_halo(velocity, theta_field, vapour)
    state_new, radius_new, outgoing = local_step(
        pad,
        yhalo,
        *(a.reshape(TILES, 8, 128) for a in (radius, multiplicity, solute)),
        counts,
        leave_slot.reshape(BLOCKS, 128),
        leave_dir.reshape(BLOCKS, 128),
    )
    arrivals = exchange_droplets(outgoing)
    return (state_new, radius_new.reshape(radius.shape), arrivals.reshape(3, 4, 1, 1, CAP))


def solution(mesh):
    in_specs = (
        P(None, None, "gx", "gy"),
        P(None, "gx", "gy"),
        P(None, "gx", "gy"),
        P(None, None, "gx", "gy"),
        P(None, None, "gx", "gy"),
        P(None, None, "gx", "gy"),
        P(None, "gx", "gy"),
        P("gx", "gy", None),
        P("gx", "gy", None),
    )
    out_specs = (
        P(None, None, "gx", "gy"),
        P(None, None, "gx", "gy"),
        P(None, None, "gx", "gy", None),
    )
    return jax.shard_map(
        per_device, mesh=mesh, in_specs=in_specs, out_specs=out_specs, check_vma=False
    )
```

```python
import functools

import jax
import jax.numpy as jnp
from jax import lax
from jax.experimental import pallas as pl
from jax.experimental.pallas import tpu as pltpu
from jax.sharding import PartitionSpec as P

MESH = pl.DeviceIdType.MESH
VMEM_SPEC = pl.BlockSpec(memory_space=pltpu.VMEM)
ANY_SPEC = pl.BlockSpec(memory_space=pl.ANY)
HBM_SPEC = pl.BlockSpec(memory_space=pltpu.HBM)

CX, CY, NZ, SLOTS, CAP, MIG = 16, 128, 16, 5, 2048, 8192
TILES = SLOTS * NZ * 2
BLOCKS = MIG // 128
BINS = 64
HALF = 16
GROUP = 6

TIME_STEP = 0.5
DIFFUSION = 0.05
BUOYANCY = 0.0327
SATURATION = 10.0
SAT_SLOPE = 0.06
GROWTH = 20.0
CURVATURE = 1.0
HYGROSCOPY = 1.0
FLOOR_SQUARE = 0.25
UPTAKE = 0.001
HEATING = 2.5

F32, BF16, I32 = jnp.float32, jnp.bfloat16, jnp.int32


def iota(shape, dim):
    return lax.broadcasted_iota(I32, shape, dim)


def ring(axis):
    count = lax.axis_size(axis)
    me = lax.axis_index(axis)
    return {axis: lax.rem(me + 1, count)}, {axis: lax.rem(me + count - 1, count)}


def greet(neighbours):
    for there in neighbours:
        pl.semaphore_signal(
            pltpu.get_barrier_semaphore(), inc=1, device_id=there, device_id_type=MESH
        )


def greeted(neighbours):
    pl.semaphore_wait(pltpu.get_barrier_semaphore(), len(neighbours))


def iota16(shape):
    return iota(shape, 0).astype(F32).astype(BF16)


def row16(tile, q, rows):
    return jnp.broadcast_to(tile[q : q + 1], (rows, 128)).astype(BF16)


def hot16(hit):
    return jnp.where(hit, jnp.ones(hit.shape, BF16), jnp.zeros(hit.shape, BF16))


def to_bf16(mask):
    return jnp.where(mask, 1.0, 0.0).astype(BF16)


NT = (((1,), (1,)), ((), ()))
NN = (((1,), (0,)), ((), ()))


def dot(a, b, dims=NN):
    return lax.dot_general(a, b, dims, preferred_element_type=F32)


def entry_codes(slots, ways, codes):
    before = iota((128, 128), 0) < iota((128, 128), 1)
    counter = jnp.concatenate([to_bf16(before), jnp.ones((128, 128), BF16)], 1)
    slot = slots[...]
    valid = slot >= 0
    way = jnp.where(valid, ways[...], -1)
    marks = [jnp.where(way == d, 1.0, 0.0) for d in range(4)]
    inside = dot(jnp.concatenate(marks, 0).astype(BF16), counter)
    earlier = to_bf16(iota((BLOCKS, BLOCKS), 1) < iota((BLOCKS, BLOCKS), 0))
    rank = jnp.zeros((BLOCKS, 128), F32)
    for d in range(4):
        block = inside[d * BLOCKS : (d + 1) * BLOCKS]
        offset = dot(earlier, block[:, 128:].astype(BF16))
        rank = rank + marks[d] * (block[:, :128] + offset)
    rank = rank.astype(I32)
    row = lax.shift_right_logical(slot, 7)
    inner = row & 7
    place_row = (way << 3) + (lax.shift_right_logical(rank, 7) & 7)
    column = (rank & 127) + (lax.shift_right_logical(rank, 10) << 7)
    codes[0] = jnp.where(valid, lax.shift_right_logical(row, 3) + 1, 0).astype(F32)
    codes[1] = column.astype(F32)
    codes[2] = (inner + (place_row << 3)).astype(F32)
    codes[3] = jnp.where(valid, slot & 127, -1).astype(F32)
    return counter


def spread_row(bins8, code8, q, spread):
    hit = iota16((BINS, 128)) == row16(bins8, q, BINS)
    for n in range(3):
        value = row16(code8[n], q, BINS)
        spread[n * BINS : (n + 1) * BINS, q * 128 : q * 128 + 128] = jnp.where(
            hit, value, jnp.zeros_like(value)
        )


def bin_lists(slots, ways, codes, bin_of, table, most, hots, spread):
    counter = entry_codes(slots, ways, codes)
    table[...] = jnp.zeros_like(table)

    def turn(t, carry):
        tile = pl.ds(pl.multiple_of(t * 8, 8), 8)
        lane8 = codes[3, tile]
        code8 = [codes[n, tile] for n in range(3)]
        found = []
        for q in range(8):
            hit = iota((128, 128), 0).astype(F32) == lane8[q : q + 1]
            hot = to_bf16(hit)
            hots[:, q * 128 : q * 128 + 128] = hot
            counted = dot(hot, counter)
            found.append(
                jnp.sum(jnp.where(hit, counted[:, :128] + carry, 0.0), axis=0, keepdims=True)
            )
            carry = carry + counted[:, 128:]
        bins8 = jnp.concatenate(found, 0)
        bin_of[tile] = bins8
        bins8 = jnp.minimum(bins8, float(BINS))
        for q in range(8):
            spread_row(bins8, code8, q, spread)
        table[...] += dot(spread[...], hots[...], NT)
        return carry

    most[...] = lax.fori_loop(0, BLOCKS // 8, turn, jnp.zeros((128, 128), F32))


def halo_kernel(
    vel, theta, vap, radius_in, mult_in, sol_in, counts_in, slots_in, ways_in,
    pad, yhalo, radius, mult, sol, counts, codes, bin_of, table, most,
    packed, landed, slots, ways, hots, spread, local_sem, send_sem, recv_sem,
):
    east, west = ring("gx")
    north, south = ring("gy")
    neighbours = (east, west, north, south)
    greet(neighbours)
    pairs = (
        (vel, pad.at[0:3, :, 8:24, :]),
        (theta, pad.at[3, :, 8:24, :]),
        (vap, pad.at[4, :, 8:24, :]),
        (slots_in, slots),
        (ways_in, ways),
        (radius_in, radius),
        (mult_in, mult),
        (sol_in, sol),
        (counts_in, counts),
    )
    loads = [
        pltpu.make_async_copy(source, target, local_sem.at[number])
        for number, (source, target) in enumerate(pairs)
    ]
    for copy in loads:
        copy.start()
    for copy in loads[:3]:
        copy.wait()

    turned = lax.rem(iota((16, 128), 1) + 3, 128)
    number = turned // GROUP

    def pack(quarter, _):
        total = jnp.zeros((16, 128), F32)
        for inner_level in range(4):
            for f in range(5):
                g = inner_level * 5 + f
                value = pad[f, quarter * 4 + inner_level, 8:24]
                if g:
                    value = pltpu.roll(value, GROUP * g, 1)
                total = jnp.where(number == g, value, total)
        packed[quarter] = total
        return _

    lax.fori_loop(0, 4, pack, 0)
    greeted(neighbours)
    routes = (
        (packed, landed.at[0], north),
        (packed, landed.at[1], south),
        (pad.at[:, :, 21:24, :], pad.at[:, :, 5:8, :], east),
        (pad.at[:, :, 8:11, :], pad.at[:, :, 24:27, :], west),
    )
    sends = [
        pltpu.make_async_remote_copy(
            src_ref=source,
            dst_ref=target,
            send_sem=send_sem.at[number],
            recv_sem=recv_sem.at[number],
            device_id=there,
            device_id_type=MESH,
        )
        for number, (source, target, there) in enumerate(routes)
    ]
    for copy in sends:
        copy.start()
    for copy in loads[3:5]:
        copy.wait()
    bin_lists(slots, ways, codes, bin_of, table, most, hots, spread)
    for copy in loads[5:]:
        copy.wait()
    sends[0].wait_recv()
    sends[1].wait_recv()
    from_south = turned - number * GROUP < 3
    for quarter in range(4):
        yhalo[quarter] = jnp.where(from_south, landed[0, quarter], landed[1, quarter])
    sends[2].wait_recv()
    sends[3].wait_recv()
    for copy in sends:
        copy.wait_send()


def exchange_halo(velocity, theta_field, vapour, radius, multiplicity, solute, counts, slots, ways):
    drops = jax.ShapeDtypeStruct((TILES, 8, 128), F32)
    return pl.pallas_call(
        halo_kernel,
        out_shape=(
            jax.ShapeDtypeStruct((5, NZ, 32, CY), F32),
            jax.ShapeDtypeStruct((4, 16, 128), F32),
            drops,
            drops,
            drops,
            jax.ShapeDtypeStruct((NZ, CX, CY), I32),
            jax.ShapeDtypeStruct((4, BLOCKS, 128), F32),
            jax.ShapeDtypeStruct((BLOCKS, 128), F32),
            jax.ShapeDtypeStruct((3 * BINS, 128), F32),
            jax.ShapeDtypeStruct((128, 128), F32),
        ),
        in_specs=[HBM_SPEC] * 9,
        out_specs=(VMEM_SPEC,) * 10,
        scratch_shapes=[
            pltpu.VMEM((4, 16, 128), F32),
            pltpu.VMEM((2, 4, 16, 128), F32),
            pltpu.VMEM((BLOCKS, 128), I32),
            pltpu.VMEM((BLOCKS, 128), I32),
            pltpu.VMEM((128, 1024), BF16),
            pltpu.VMEM((3 * BINS, 1024), BF16),
            pltpu.SemaphoreType.DMA((9,)),
            pltpu.SemaphoreType.DMA((4,)),
            pltpu.SemaphoreType.DMA((4,)),
        ],
        compiler_params=pltpu.CompilerParams(
            collective_id=0, has_side_effects=True, vmem_limit_bytes=24 << 20
        ),
    )(velocity, theta_field, vapour, radius, multiplicity, solute, counts, slots, ways)


def line_weights():
    apart = iota((128, 128), 0) - iota((128, 128), 1)

    def weights(far):
        size = jnp.abs(far)
        sign = jnp.where(far < 0, -1.0, 1.0)
        centred = jnp.where(size == 1, 45.0, jnp.where(size == 2, -9.0, jnp.where(size == 3, 1.0, 0.0)))
        damping = jnp.where(
            size == 0, -20.0,
            jnp.where(size == 1, 15.0, jnp.where(size == 2, -6.0, jnp.where(size == 3, 1.0, 0.0))),
        )
        beside = jnp.where(size == 1, 1.0, 0.0)
        return jnp.concatenate([centred * sign, damping, beside], 1)

    own = weights(apart)
    halo = weights(apart + 128) + weights(apart - 128)
    return jnp.concatenate([own, own, halo, halo], 0).astype(BF16)


def physics(pad, yhalo, radius, mult, sol, counts, state, rnew, grown, lines, along, weights, done):
    weights[...] = line_weights()

    def lines_turn(quarter, _):
        for inner_level in range(4):
            for f in range(5):
                g = inner_level * 5 + f
                edge = yhalo[quarter]
                if g:
                    edge = pltpu.roll(edge, 128 - GROUP * g, 1)
                for position, value in enumerate((pad[f, quarter * 4 + inner_level, 8:24], edge)):
                    high = value.astype(BF16)
                    low = (value - high.astype(F32)).astype(BF16)
                    rows = slice(16 * g, 16 * g + 16)
                    lines[rows, 256 * position : 256 * position + 128] = high
                    lines[rows, 256 * position + 128 : 256 * position + 256] = low
        along[quarter] = dot(lines[...], weights[...])
        return _

    lax.fori_loop(0, 4, lines_turn, 0)

    def quarter_turn(quarter, _):
        for inner_level in range(4):
            k = quarter * 4 + inner_level
            above = jnp.minimum(k + 1, NZ - 1)
            below = jnp.maximum(k - 1, 0)
            for half in range(2):
                base = 8 + 8 * half
                rows = slice(8 * half, 8 * half + 8)
                u = pad[0, k, base : base + 8] * (-TIME_STEP / 60.0)
                v = pad[1, k, base : base + 8] * (-TIME_STEP / 60.0)
                w = pad[2, k, base : base + 8]
                lift = DIFFUSION * TIME_STEP - w * (0.5 * TIME_STEP)
                sink = DIFFUSION * TIME_STEP + w * (0.5 * TIME_STEP)
                u_size, v_size = jnp.abs(u), jnp.abs(v)
                moved = []
                for f in range(5):
                    mid = pad[f, k, base : base + 8]
                    p1, m1, p2, m2, p3, m3 = (
                        pad[f, k, base + d : base + d + 8] for d in (1, -1, 2, -2, 3, -3)
                    )
                    g = 16 * (inner_level * 5 + f) + 8 * half
                    y_centred, y_damping, y_beside = (
                        along[quarter, g : g + 8, 128 * n : 128 * n + 128] for n in range(3)
                    )
                    s1 = p1 + m1
                    total = mid + u * (45.0 * (p1 - m1) - 9.0 * (p2 - m2) + (p3 - m3))
                    total = total + u_size * (15.0 * s1 - 6.0 * (p2 + m2) + (p3 + m3) - 20.0 * mid)
                    total = total + v * y_centred + v_size * y_damping
                    total = total + (DIFFUSION * TIME_STEP) * (s1 + y_beside - 6.0 * mid)
                    up = pad[f, above, base : base + 8]
                    down = pad[f, below, base : base + 8]
                    total = total + lift * up + sink * down
                    if f == 2:
                        total = total + (TIME_STEP * BUOYANCY) * pad[3, k, base : base + 8]
                    moved.append(total)
                supersat = moved[4] * (jnp.exp(-SAT_SLOPE * moved[3]) * (1.0 / SATURATION)) - 1.0
                alive_count = counts[k, rows]
                condensed = jnp.zeros((8, 128), F32)
                for s in range(SLOTS):
                    tile = (s * NZ + k) * 2 + half
                    r = radius[tile]
                    inv = 1.0 / r
                    r2 = r * r
                    square = r2 + GROWTH * (
                        supersat - CURVATURE * inv + (HYGROSCOPY * sol[tile]) * (inv * inv * inv)
                    )
                    square = jnp.maximum(square, FLOOR_SQUARE)
                    new = jnp.sqrt(square)
                    alive = s < alive_count
                    grown[tile] = new
                    rnew[tile] = jnp.where(alive, new, 0.0)
                    condensed = condensed + jnp.where(
                        alive, mult[tile] * (square * new - r2 * r), 0.0
                    )
                state[0, k, rows] = moved[0]
                state[1, k, rows] = moved[1]
                state[2, k, rows] = moved[2]
                state[3, k, rows] = moved[3] + (HEATING * UPTAKE) * condensed
                state[4, k, rows] = moved[4] - UPTAKE * condensed
        done(quarter)
        return _

    lax.fori_loop(0, 4, quarter_turn, 0)


def pick_turn(chunk, codes, bin_of, table, hots, spread, grown, mult, sol, rnew, values, places, rows_hot, out_acc):
    @pl.when(chunk > 0)
    def _():
        table[...] = jnp.zeros_like(table)

        def spread_turn(t, _):
            tile = pl.ds(pl.multiple_of(t * 8, 8), 8)
            low = (chunk * BINS).astype(F32)
            bins8 = jnp.maximum(jnp.minimum(bin_of[tile] - low, float(BINS)), -1.0)
            lane8 = codes[3, tile]
            code8 = [codes[n, tile] for n in range(3)]
            for q in range(8):
                hots[:, q * 128 : q * 128 + 128] = to_bf16(
                    iota((128, 128), 0).astype(F32) == lane8[q : q + 1]
                )
                spread_row(bins8, code8, q, spread)
            table[...] += dot(spread[...], hots[...], NT)
            return _

        lax.fori_loop(0, BLOCKS // 8, spread_turn, 0)

    first = table[0:BINS].astype(I32)
    third = table[2 * BINS : 3 * BINS].astype(I32)
    group = first - 1
    inner = third & 7
    places[0] = jnp.where(first > 0, lax.shift_right_logical(third, 3), -1).astype(F32)
    places[1] = table[BINS : 2 * BINS]

    parts = BINS // 8
    groups = [group[8 * m : 8 * m + 8] for m in range(parts)]
    inners = [inner[8 * m : 8 * m + 8] for m in range(parts)]
    bits = [jnp.left_shift(1, inners[m]) for m in range(parts)]
    sublane = iota((8, 128), 0)

    def gather_turn(j, kept):
        sources = (grown[j], mult[j], sol[j])
        kept = list(kept)
        marked = jnp.zeros((8, 128), I32)
        for m in range(parts):
            hit = groups[m] == j
            marked = marked | jnp.where(hit, bits[m], 0)
            for n in range(3):
                got = jnp.take_along_axis(sources[n], inners[m], axis=0, mode="promise_in_bounds")
                kept[n * parts + m] = jnp.where(hit, got, kept[n * parts + m])
        marked = marked | pltpu.roll(marked, 4, 0)
        marked = marked | pltpu.roll(marked, 2, 0)
        marked = marked | pltpu.roll(marked, 1, 0)
        left = lax.shift_right_logical(marked, sublane) & 1
        rnew[j] = jnp.where(left == 1, 0.0, rnew[j])
        return tuple(kept)

    kept = lax.fori_loop(
        0, TILES, gather_turn, tuple(jnp.zeros((8, 128), F32) for _ in range(3 * parts)), unroll=4
    )
    for n in range(3):
        for m in range(parts):
            values[n, 8 * m : 8 * m + 8] = kept[n * parts + m]

    def place_turn(t, _):
        tile = pl.ds(pl.multiple_of(t * 8, 8), 8)
        row8, column8 = places[0, tile], places[1, tile]
        high = [values[n, tile].astype(BF16).astype(F32) for n in range(3)]
        low = [values[n, tile] - high[n] for n in range(3)]
        for q in range(8):
            columns = slice(q * 128, q * 128 + 128)
            hit = iota16((2 * HALF, 128)) == row16(row8, q, 2 * HALF)
            for n, piece in enumerate(high + low):
                value = row16(piece, q, 2 * HALF)
                rows_hot[2 * HALF * n : 2 * HALF * (n + 1), columns] = jnp.where(
                    hit, value, jnp.zeros_like(value)
                )
            rows_hot[12 * HALF :, columns] = hot16(iota16((256, 128)) == row16(column8, q, 256))
        out_acc[...] += dot(rows_hot[: 12 * HALF], rows_hot[12 * HALF :], NT)
        return _

    lax.fori_loop(0, BINS // 8, place_turn, 0)


def local_kernel(
    pad, yhalo, radius, mult, sol, counts, codes, bin_of, table_in, most,
    state_out, rnew_out, outgoing,
    state, rnew, grown, lines, along, weights, table, hots, spread, values, places, rows_hot, out_acc, sems,
):
    state_saves = [
        pltpu.make_async_copy(
            state.at[:, 4 * quarter : 4 * quarter + 4], state_out.at[:, 4 * quarter : 4 * quarter + 4], sems.at[quarter]
        )
        for quarter in range(4)
    ]

    physics(
        pad, yhalo, radius, mult, sol, counts, state, rnew, grown, lines, along, weights, lambda quarter: None
    )
    for copy in state_saves:
        copy.start()
    table[...] = table_in[...]
    out_acc[...] = jnp.zeros_like(out_acc)

    def turn(chunk, _):
        pick_turn(
            chunk, codes, bin_of, table, hots, spread, grown, mult, sol, rnew, values, places, rows_hot, out_acc
        )
        return _

    chunks = (jnp.max(most[...]).astype(I32) + BINS - 1) // BINS
    lax.fori_loop(0, chunks, turn, 0)
    rnew_save = pltpu.make_async_copy(rnew, rnew_out, sems.at[4])
    rnew_save.start()
    for d in range(4):
        for n in range(3):
            first = n * 2 * HALF + d * 8
            total = out_acc[first : first + 8] + out_acc[first + 6 * HALF : first + 6 * HALF + 8]
            outgoing[d, n, 0:8] = total[:, :128]
            outgoing[d, n, 8:16] = total[:, 128:]
    for copy in state_saves:
        copy.wait()
    rnew_save.wait()


def local_step(*operands):
    return pl.pallas_call(
        local_kernel,
        out_shape=(
            jax.ShapeDtypeStruct((5, NZ, CX, CY), F32),
            jax.ShapeDtypeStruct((TILES, 8, 128), F32),
            jax.ShapeDtypeStruct((4, 3, CAP // 128, 128), F32),
        ),
        in_specs=[VMEM_SPEC] * 10,
        out_specs=(HBM_SPEC, HBM_SPEC, VMEM_SPEC),
        scratch_shapes=[
            pltpu.VMEM((5, NZ, CX, CY), F32),
            pltpu.VMEM((TILES, 8, 128), F32),
            pltpu.VMEM((TILES, 8, 128), F32),
            pltpu.VMEM((320, 512), BF16),
            pltpu.VMEM((4, 320, 384), F32),
            pltpu.VMEM((512, 384), BF16),
            pltpu.VMEM((3 * BINS, 128), F32),
            pltpu.VMEM((128, 1024), BF16),
            pltpu.VMEM((3 * BINS, 1024), BF16),
            pltpu.VMEM((3, BINS, 128), F32),
            pltpu.VMEM((2, BINS, 128), F32),
            pltpu.VMEM((12 * HALF + 256, 1024), BF16),
            pltpu.VMEM((12 * HALF, 256), F32),
            pltpu.SemaphoreType.DMA((5,)),
        ],
        compiler_params=pltpu.CompilerParams(vmem_limit_bytes=24 << 20),
    )(*operands)


def droplet_kernel(outgoing, arrivals, send_sem, recv_sem):
    east, west = ring("gx")
    north, south = ring("gy")
    ways = (east, west, north, south)
    greet(ways)
    greeted(ways)
    sends = [
        pltpu.make_async_remote_copy(
            src_ref=outgoing.at[d],
            dst_ref=arrivals.at[:, d],
            send_sem=send_sem.at[d],
            recv_sem=recv_sem.at[d],
            device_id=there,
            device_id_type=MESH,
        )
        for d, there in enumerate(ways)
    ]
    for copy in sends:
        copy.start()
    for copy in sends:
        copy.wait()


def exchange_droplets(outgoing):
    return pl.pallas_call(
        droplet_kernel,
        out_shape=jax.ShapeDtypeStruct((3, 4, CAP // 128, 128), F32),
        in_specs=[ANY_SPEC],
        out_specs=ANY_SPEC,
        scratch_shapes=[pltpu.SemaphoreType.DMA((4,)), pltpu.SemaphoreType.DMA((4,))],
        compiler_params=pltpu.CompilerParams(
            collective_id=1, has_side_effects=True, vmem_limit_bytes=4 << 20
        ),
    )(outgoing)


def store_kernel(source, target, sem):
    copy = pltpu.make_async_copy(source, target, sem)
    copy.start()
    copy.wait()


def store(arrivals):
    return pl.pallas_call(
        store_kernel,
        out_shape=jax.ShapeDtypeStruct(arrivals.shape, F32),
        in_specs=[ANY_SPEC],
        out_specs=HBM_SPEC,
        scratch_shapes=[pltpu.SemaphoreType.DMA],
        compiler_params=pltpu.CompilerParams(vmem_limit_bytes=4 << 20),
    )(arrivals)


def per_device(
    velocity, theta_field, vapour, radius, multiplicity, solute, counts, leave_slot, leave_dir
):
    drops = (a.reshape(TILES, 8, 128) for a in (radius, multiplicity, solute))
    lists = (a.reshape(BLOCKS, 128) for a in (leave_slot, leave_dir))
    inputs = (velocity, theta_field, vapour, *drops, counts, *lists)
    ready = exchange_halo(*(pltpu.with_memory_space_constraint(a, pltpu.HBM) for a in inputs))
    state_new, radius_new, outgoing = local_step(*ready)
    arrivals = store(exchange_droplets(outgoing))
    return (state_new, radius_new.reshape(radius.shape), arrivals.reshape(3, 4, 1, 1, CAP))


def solution(mesh):
    in_specs = (
        P(None, None, "gx", "gy"),
        P(None, "gx", "gy"),
        P(None, "gx", "gy"),
        P(None, None, "gx", "gy"),
        P(None, None, "gx", "gy"),
        P(None, None, "gx", "gy"),
        P(None, "gx", "gy"),
        P("gx", "gy", None),
        P("gx", "gy", None),
    )
    out_specs = (
        P(None, None, "gx", "gy"),
        P(None, None, "gx", "gy"),
        P(None, None, "gx", "gy", None),
    )
    return jax.shard_map(
        per_device, mesh=mesh, in_specs=in_specs, out_specs=out_specs, check_vma=False
    )
```

```python
import functools

import jax
import jax.numpy as jnp
from jax import lax
from jax.experimental import pallas as pl
from jax.experimental.pallas import tpu as pltpu
from jax.sharding import PartitionSpec as P

MESH = pl.DeviceIdType.MESH
VMEM_SPEC = pl.BlockSpec(memory_space=pltpu.VMEM)
ANY_SPEC = pl.BlockSpec(memory_space=pl.ANY)
HBM_SPEC = pl.BlockSpec(memory_space=pltpu.HBM)

CX, CY, NZ, SLOTS, CAP, MIG = 16, 128, 16, 5, 2048, 8192
TILES = SLOTS * NZ * 2
BLOCKS = MIG // 128
BINS = 64
HALF = 16
GROUP = 6

TIME_STEP = 0.5
DIFFUSION = 0.05
BUOYANCY = 0.0327
SATURATION = 10.0
SAT_SLOPE = 0.06
GROWTH = 20.0
CURVATURE = 1.0
HYGROSCOPY = 1.0
FLOOR_SQUARE = 0.25
UPTAKE = 0.001
HEATING = 2.5

F32, BF16, I32 = jnp.float32, jnp.bfloat16, jnp.int32


def iota(shape, dim):
    return lax.broadcasted_iota(I32, shape, dim)


def ring(axis):
    count = lax.axis_size(axis)
    me = lax.axis_index(axis)
    return {axis: lax.rem(me + 1, count)}, {axis: lax.rem(me + count - 1, count)}


def greet(neighbours):
    for there in neighbours:
        pl.semaphore_signal(
            pltpu.get_barrier_semaphore(), inc=1, device_id=there, device_id_type=MESH
        )


def greeted(neighbours):
    pl.semaphore_wait(pltpu.get_barrier_semaphore(), len(neighbours))


def iota16(shape):
    return iota(shape, 0).astype(F32).astype(BF16)


def row16(tile, q, rows):
    return jnp.broadcast_to(tile[q : q + 1], (rows, 128)).astype(BF16)


def hot16(hit):
    return jnp.where(hit, jnp.ones(hit.shape, BF16), jnp.zeros(hit.shape, BF16))


def to_bf16(mask):
    return jnp.where(mask, 1.0, 0.0).astype(BF16)


NT = (((1,), (1,)), ((), ()))
NN = (((1,), (0,)), ((), ()))


def dot(a, b, dims=NN):
    return lax.dot_general(a, b, dims, preferred_element_type=F32)


def entry_codes(slots, ways, codes):
    before = iota((128, 128), 0) < iota((128, 128), 1)
    counter = jnp.concatenate([to_bf16(before), jnp.ones((128, 128), BF16)], 1)
    slot = slots[...]
    valid = slot >= 0
    way = jnp.where(valid, ways[...], -1)
    marks = [jnp.where(way == d, 1.0, 0.0) for d in range(4)]
    inside = dot(jnp.concatenate(marks, 0).astype(BF16), counter)
    earlier = to_bf16(iota((BLOCKS, BLOCKS), 1) < iota((BLOCKS, BLOCKS), 0))
    rank = jnp.zeros((BLOCKS, 128), F32)
    for d in range(4):
        block = inside[d * BLOCKS : (d + 1) * BLOCKS]
        offset = dot(earlier, block[:, 128:].astype(BF16))
        rank = rank + marks[d] * (block[:, :128] + offset)
    rank = rank.astype(I32)
    row = lax.shift_right_logical(slot, 7)
    inner = row & 7
    place_row = (way << 3) + (lax.shift_right_logical(rank, 7) & 7)
    column = (rank & 127) + (lax.shift_right_logical(rank, 10) << 7)
    codes[0] = jnp.where(valid, lax.shift_right_logical(row, 3) + 1, 0).astype(F32)
    codes[1] = column.astype(F32)
    codes[2] = (inner + (place_row << 3)).astype(F32)
    codes[3] = jnp.where(valid, slot & 127, -1).astype(F32)
    return counter


def spread_row(number, code8, q):
    hit = iota16((BINS, 128)) == jnp.broadcast_to(number, (BINS, 128)).astype(BF16)
    spread = []
    for n in range(3):
        value = row16(code8[n], q, BINS)
        spread.append(jnp.where(hit, value, jnp.zeros_like(value)))
    return jnp.concatenate(spread, 0)


def bin_lists(slots, ways, codes, bin_of, table, most):
    counter = entry_codes(slots, ways, codes)
    table[...] = jnp.zeros_like(table)

    def turn(t, carry):
        tile = pl.ds(pl.multiple_of(t * 8, 8), 8)
        lane8 = codes[3, tile]
        code8 = [codes[n, tile] for n in range(3)]
        found, hots, spread = [], [], []
        for q in range(8):
            hit = iota((128, 128), 0).astype(F32) == lane8[q : q + 1]
            hots.append(to_bf16(hit))
            counted = dot(hots[-1], counter)
            number = jnp.sum(
                jnp.where(hit, counted[:, :128] + carry, 0.0), axis=0, keepdims=True
            )
            carry = carry + counted[:, 128:]
            found.append(number)
            spread.append(spread_row(jnp.minimum(number, float(BINS)), code8, q))
        bin_of[tile] = jnp.concatenate(found, 0)
        table[...] += dot(jnp.concatenate(spread, 1), jnp.concatenate(hots, 1), NT)
        return carry

    most[...] = lax.fori_loop(0, BLOCKS // 8, turn, jnp.zeros((128, 128), F32), unroll=8)


PARTS = BINS // 8


def read_table(table):
    first = table[0:BINS].astype(I32)
    third = table[2 * BINS : 3 * BINS].astype(I32)
    group = first - 1
    inner = third & 7
    groups = [group[8 * m : 8 * m + 8] for m in range(PARTS)]
    inners = [inner[8 * m : 8 * m + 8] for m in range(PARTS)]
    place_row = jnp.where(first > 0, lax.shift_right_logical(third, 3), -1).astype(F32)
    return groups, inners, place_row, table[BINS : 2 * BINS]


def gather(groups, inners, sources, values, first, mark, unroll):
    bits = [jnp.left_shift(1, inners[m]) for m in range(PARTS)]
    sublane = iota((8, 128), 0)
    count = len(sources)

    def turn(j, kept):
        tiles = [source[j] for source in sources]
        kept = list(kept)
        marked = jnp.zeros((8, 128), I32)
        for m in range(PARTS):
            hit = groups[m] == j
            if mark is not None:
                marked = marked | jnp.where(hit, bits[m], 0)
            for n in range(count):
                got = jnp.take_along_axis(tiles[n], inners[m], axis=0, mode="promise_in_bounds")
                kept[n * PARTS + m] = jnp.where(hit, got, kept[n * PARTS + m])
        if mark is not None:
            marked = marked | pltpu.roll(marked, 4, 0)
            marked = marked | pltpu.roll(marked, 2, 0)
            marked = marked | pltpu.roll(marked, 1, 0)
            mark(j, (lax.shift_right_logical(marked, sublane) & 1) == 1)
        return tuple(kept)

    start = tuple(jnp.zeros((8, 128), F32) for _ in range(count * PARTS))
    kept = lax.fori_loop(0, TILES, turn, start, unroll=unroll)
    for n in range(count):
        for m in range(PARTS):
            values[first + n, 8 * m : 8 * m + 8] = kept[n * PARTS + m]


def place_bins(tile_of, places, out_acc, unroll):
    def turn(t, _):
        tile = pl.ds(pl.multiple_of(t * 8, 8), 8)
        row8, column8 = places[0, tile], places[1, tile]
        whole = tile_of(tile)
        high = [value.astype(BF16).astype(F32) for value in whole]
        low = [value - part for value, part in zip(whole, high)]
        rows, columns = [], []
        for q in range(8):
            hit = iota16((2 * HALF, 128)) == row16(row8, q, 2 * HALF)
            parts = []
            for piece in high + low:
                value = row16(piece, q, 2 * HALF)
                parts.append(jnp.where(hit, value, jnp.zeros_like(value)))
            rows.append(jnp.concatenate(parts, 0))
            columns.append(hot16(iota16((256, 128)) == row16(column8, q, 256)))
        out_acc[...] += dot(jnp.concatenate(rows, 1), jnp.concatenate(columns, 1), NT)
        return _

    lax.fori_loop(0, PARTS, turn, 0, unroll=unroll)


def halo_kernel(
    vel, theta, vap, radius_in, mult_in, sol_in, counts_in, slots_in, ways_in,
    pad, yhalo, radius, mult, sol, counts, codes, bin_of, table, most, values, places, stays,
    packed, landed, slots, ways, local_sem, send_sem, recv_sem,
):
    east, west = ring("gx")
    north, south = ring("gy")
    neighbours = (east, west, north, south)
    greet(neighbours)
    pairs = (
        (vel, pad.at[0:3, :, 8:24, :]),
        (theta, pad.at[3, :, 8:24, :]),
        (vap, pad.at[4, :, 8:24, :]),
        (slots_in, slots),
        (ways_in, ways),
        (radius_in, radius),
        (mult_in, mult),
        (sol_in, sol),
        (counts_in, counts),
    )
    loads = [
        pltpu.make_async_copy(source, target, local_sem.at[number])
        for number, (source, target) in enumerate(pairs)
    ]
    for copy in loads:
        copy.start()
    for copy in loads[:3]:
        copy.wait()

    turned = lax.rem(iota((16, 128), 1) + 3, 128)
    number = turned // GROUP

    def pack(quarter, _):
        total = jnp.zeros((16, 128), F32)
        for inner_level in range(4):
            for f in range(5):
                g = inner_level * 5 + f
                value = pad[f, quarter * 4 + inner_level, 8:24]
                if g:
                    value = pltpu.roll(value, GROUP * g, 1)
                total = jnp.where(number == g, value, total)
        packed[quarter] = total
        return _

    lax.fori_loop(0, 4, pack, 0)
    greeted(neighbours)
    routes = (
        (packed, landed.at[0], north),
        (packed, landed.at[1], south),
        (pad.at[:, :, 21:24, :], pad.at[:, :, 5:8, :], east),
        (pad.at[:, :, 8:11, :], pad.at[:, :, 24:27, :], west),
    )
    sends = [
        pltpu.make_async_remote_copy(
            src_ref=source,
            dst_ref=target,
            send_sem=send_sem.at[number],
            recv_sem=recv_sem.at[number],
            device_id=there,
            device_id_type=MESH,
        )
        for number, (source, target, there) in enumerate(routes)
    ]
    for copy in sends:
        copy.start()
    for copy in loads[3:5]:
        copy.wait()
    bin_lists(slots, ways, codes, bin_of, table, most)
    for copy in loads[5:]:
        copy.wait()
    groups, inners, places[0], places[1] = read_table(table)

    def mark(j, left):
        stays[j] = jnp.where(left, 0.0, 1.0)

    gather(groups, inners, (mult, sol), values, 0, mark, 8)
    sends[0].wait_recv()
    sends[1].wait_recv()
    from_south = turned - number * GROUP < 3
    for quarter in range(4):
        yhalo[quarter] = jnp.where(from_south, landed[0, quarter], landed[1, quarter])
    sends[2].wait_recv()
    sends[3].wait_recv()
    for copy in sends:
        copy.wait_send()


def exchange_halo(velocity, theta_field, vapour, radius, multiplicity, solute, counts, slots, ways):
    drops = jax.ShapeDtypeStruct((TILES, 8, 128), F32)
    return pl.pallas_call(
        halo_kernel,
        out_shape=(
            jax.ShapeDtypeStruct((5, NZ, 32, CY), F32),
            jax.ShapeDtypeStruct((4, 16, 128), F32),
            drops,
            drops,
            drops,
            jax.ShapeDtypeStruct((NZ, CX, CY), I32),
            jax.ShapeDtypeStruct((4, BLOCKS, 128), F32),
            jax.ShapeDtypeStruct((BLOCKS, 128), F32),
            jax.ShapeDtypeStruct((3 * BINS, 128), F32),
            jax.ShapeDtypeStruct((128, 128), F32),
            jax.ShapeDtypeStruct((2, BINS, 128), F32),
            jax.ShapeDtypeStruct((2, BINS, 128), F32),
            drops,
        ),
        in_specs=[HBM_SPEC] * 9,
        out_specs=(VMEM_SPEC,) * 13,
        scratch_shapes=[
            pltpu.VMEM((4, 16, 128), F32),
            pltpu.VMEM((2, 4, 16, 128), F32),
            pltpu.VMEM((BLOCKS, 128), I32),
            pltpu.VMEM((BLOCKS, 128), I32),
            pltpu.SemaphoreType.DMA((9,)),
            pltpu.SemaphoreType.DMA((4,)),
            pltpu.SemaphoreType.DMA((4,)),
        ],
        compiler_params=pltpu.CompilerParams(
            collective_id=0, has_side_effects=True, vmem_limit_bytes=24 << 20
        ),
    )(velocity, theta_field, vapour, radius, multiplicity, solute, counts, slots, ways)


def line_weights():
    apart = iota((128, 128), 0) - iota((128, 128), 1)

    def weights(far):
        size = jnp.abs(far)
        sign = jnp.where(far < 0, -1.0, 1.0)
        centred = jnp.where(size == 1, 45.0, jnp.where(size == 2, -9.0, jnp.where(size == 3, 1.0, 0.0)))
        damping = jnp.where(
            size == 0, -20.0,
            jnp.where(size == 1, 15.0, jnp.where(size == 2, -6.0, jnp.where(size == 3, 1.0, 0.0))),
        )
        beside = jnp.where(size == 1, 1.0, 0.0)
        return jnp.concatenate([centred * sign, damping, beside], 1)

    own = weights(apart)
    halo = weights(apart + 128) + weights(apart - 128)
    return jnp.concatenate([own, own, halo, halo], 0).astype(BF16)


def physics(pad, yhalo, radius, mult, sol, counts, stays, state, rnew, grown, lines, along, weights):
    weights[...] = line_weights()

    def lines_turn(quarter):
        for inner_level in range(4):
            for f in range(5):
                g = inner_level * 5 + f
                edge = yhalo[quarter]
                if g:
                    edge = pltpu.roll(edge, 128 - GROUP * g, 1)
                for position, value in enumerate((pad[f, quarter * 4 + inner_level, 8:24], edge)):
                    high = value.astype(BF16)
                    low = (value - high.astype(F32)).astype(BF16)
                    rows = slice(16 * g, 16 * g + 16)
                    lines[quarter, rows, 256 * position : 256 * position + 128] = high
                    lines[quarter, rows, 256 * position + 128 : 256 * position + 256] = low
        along[quarter] = dot(lines[quarter], weights[...])

    def quarter_turn(quarter):
        for inner_level in range(4):
            k = quarter * 4 + inner_level
            above = min(k + 1, NZ - 1)
            below = max(k - 1, 0)
            for half in range(2):
                base = 8 + 8 * half
                rows = slice(8 * half, 8 * half + 8)
                u = pad[0, k, base : base + 8] * (-TIME_STEP / 60.0)
                v = pad[1, k, base : base + 8] * (-TIME_STEP / 60.0)
                w = pad[2, k, base : base + 8]
                lift = DIFFUSION * TIME_STEP - w * (0.5 * TIME_STEP)
                sink = DIFFUSION * TIME_STEP + w * (0.5 * TIME_STEP)
                u_size, v_size = jnp.abs(u), jnp.abs(v)
                moved = []
                for f in range(5):
                    mid = pad[f, k, base : base + 8]
                    p1, m1, p2, m2, p3, m3 = (
                        pad[f, k, base + d : base + d + 8] for d in (1, -1, 2, -2, 3, -3)
                    )
                    g = 16 * (inner_level * 5 + f) + 8 * half
                    y_centred, y_damping, y_beside = (
                        along[quarter, g : g + 8, 128 * n : 128 * n + 128] for n in range(3)
                    )
                    s1 = p1 + m1
                    total = mid + u * (45.0 * (p1 - m1) - 9.0 * (p2 - m2) + (p3 - m3))
                    total = total + u_size * (15.0 * s1 - 6.0 * (p2 + m2) + (p3 + m3) - 20.0 * mid)
                    total = total + v * y_centred + v_size * y_damping
                    total = total + (DIFFUSION * TIME_STEP) * (s1 + y_beside - 6.0 * mid)
                    up = pad[f, above, base : base + 8]
                    down = pad[f, below, base : base + 8]
                    total = total + lift * up + sink * down
                    if f == 2:
                        total = total + (TIME_STEP * BUOYANCY) * pad[3, k, base : base + 8]
                    moved.append(total)
                supersat = moved[4] * (jnp.exp(-SAT_SLOPE * moved[3]) * (1.0 / SATURATION)) - 1.0
                alive_count = counts[k, rows]
                condensed = jnp.zeros((8, 128), F32)
                for s in range(SLOTS):
                    tile = (s * NZ + k) * 2 + half
                    r = radius[tile]
                    inv = 1.0 / r
                    r2 = r * r
                    square = r2 + GROWTH * (
                        supersat - CURVATURE * inv + (HYGROSCOPY * sol[tile]) * (inv * inv * inv)
                    )
                    square = jnp.maximum(square, FLOOR_SQUARE)
                    new = jnp.sqrt(square)
                    alive = s < alive_count
                    grown[tile] = new
                    rnew[tile] = jnp.where(alive, new * stays[tile], 0.0)
                    condensed = condensed + jnp.where(
                        alive, mult[tile] * (square * new - r2 * r), 0.0
                    )
                state[0, k, rows] = moved[0]
                state[1, k, rows] = moved[1]
                state[2, k, rows] = moved[2]
                state[3, k, rows] = moved[3] + (HEATING * UPTAKE) * condensed
                state[4, k, rows] = moved[4] - UPTAKE * condensed

    lines_turn(0)
    for quarter in range(4):
        if quarter < 3:
            lines_turn(quarter + 1)
        quarter_turn(quarter)


def late_turn(chunk, codes, bin_of, table, values, places, grown, mult, sol, rnew, out_acc):
    table[...] = jnp.zeros_like(table)

    def spread_turn(t, _):
        tile = pl.ds(pl.multiple_of(t * 8, 8), 8)
        first = (chunk * BINS).astype(F32)
        bins8 = jnp.maximum(jnp.minimum(bin_of[tile] - first, float(BINS)), -1.0)
        lane8 = codes[3, tile]
        code8 = [codes[n, tile] for n in range(3)]
        hots = [to_bf16(iota((128, 128), 0).astype(F32) == lane8[q : q + 1]) for q in range(8)]
        spread = [spread_row(bins8[q : q + 1], code8, q) for q in range(8)]
        table[...] += dot(jnp.concatenate(spread, 1), jnp.concatenate(hots, 1), NT)
        return _

    lax.fori_loop(0, BLOCKS // 8, spread_turn, 0)
    groups, inners, places[0], places[1] = read_table(table)

    def mark(j, left):
        rnew[j] = jnp.where(left, 0.0, rnew[j])

    gather(groups, inners, (grown, mult, sol), values, 0, mark, 1)
    place_bins(lambda tile: [values[n, tile] for n in range(3)], places, out_acc, 1)


def local_kernel(
    pad, yhalo, radius, mult, sol, counts, codes, bin_of, table, most, stays,
    state_out, rnew_out, picked, late,
    state, rnew, grown, lines, along, weights, late_table, values, places, sems,
):
    chunks = (jnp.max(most[...]).astype(I32) + BINS - 1) // BINS
    late[...] = jnp.zeros_like(late)
    physics(pad, yhalo, radius, mult, sol, counts, stays, state, rnew, grown, lines, along, weights)

    def turn(chunk, _):
        late_turn(chunk, codes, bin_of, late_table, values, places, grown, mult, sol, rnew, late)
        return _

    lax.fori_loop(1, chunks, turn, 0)
    saves = (
        pltpu.make_async_copy(state, state_out, sems.at[0]),
        pltpu.make_async_copy(rnew, rnew_out, sems.at[1]),
    )
    for copy in saves:
        copy.start()
    groups, inners, _, _ = read_table(table)
    gather(groups, inners, (grown,), picked, 0, None, 16)
    for copy in saves:
        copy.wait()


def local_step(*operands):
    return pl.pallas_call(
        local_kernel,
        out_shape=(
            jax.ShapeDtypeStruct((5, NZ, CX, CY), F32),
            jax.ShapeDtypeStruct((TILES, 8, 128), F32),
            jax.ShapeDtypeStruct((1, BINS, 128), F32),
            jax.ShapeDtypeStruct((12 * HALF, 256), F32),
        ),
        in_specs=[VMEM_SPEC] * 11,
        out_specs=(HBM_SPEC, HBM_SPEC, VMEM_SPEC, VMEM_SPEC),
        scratch_shapes=[
            pltpu.VMEM((5, NZ, CX, CY), F32),
            pltpu.VMEM((TILES, 8, 128), F32),
            pltpu.VMEM((TILES, 8, 128), F32),
            pltpu.VMEM((4, 320, 512), BF16),
            pltpu.VMEM((4, 320, 384), F32),
            pltpu.VMEM((512, 384), BF16),
            pltpu.VMEM((3 * BINS, 128), F32),
            pltpu.VMEM((3, BINS, 128), F32),
            pltpu.VMEM((2, BINS, 128), F32),
            pltpu.SemaphoreType.DMA((2,)),
        ],
        compiler_params=pltpu.CompilerParams(vmem_limit_bytes=24 << 20),
    )(*operands)


def droplet_kernel(picked, values, places, late, arrivals, out_acc, outgoing, send_sem, recv_sem):
    east, west = ring("gx")
    north, south = ring("gy")
    ways = (east, west, north, south)
    greet(ways)
    out_acc[...] = late[...]
    place_bins(lambda tile: [picked[0, tile], values[0, tile], values[1, tile]], places, out_acc, PARTS)
    for d in range(4):
        for n in range(3):
            first = n * 2 * HALF + d * 8
            total = out_acc[first : first + 8] + out_acc[first + 6 * HALF : first + 6 * HALF + 8]
            outgoing[d, n, 0:8] = total[:, :128]
            outgoing[d, n, 8:16] = total[:, 128:]
    greeted(ways)
    sends = [
        pltpu.make_async_remote_copy(
            src_ref=outgoing.at[d],
            dst_ref=arrivals.at[:, d],
            send_sem=send_sem.at[d],
            recv_sem=recv_sem.at[d],
            device_id=there,
            device_id_type=MESH,
        )
        for d, there in enumerate(ways)
    ]
    for copy in sends:
        copy.start()
    for copy in sends:
        copy.wait()


def exchange_droplets(*operands):
    return pl.pallas_call(
        droplet_kernel,
        out_shape=jax.ShapeDtypeStruct((3, 4, CAP // 128, 128), F32),
        in_specs=[VMEM_SPEC] * 4,
        out_specs=ANY_SPEC,
        scratch_shapes=[
            pltpu.VMEM((12 * HALF, 256), F32),
            pltpu.VMEM((4, 3, CAP // 128, 128), F32),
            pltpu.SemaphoreType.DMA((4,)),
            pltpu.SemaphoreType.DMA((4,)),
        ],
        compiler_params=pltpu.CompilerParams(
            collective_id=1, has_side_effects=True, vmem_limit_bytes=16 << 20
        ),
    )(*operands)


def store_kernel(source, target, sem):
    copy = pltpu.make_async_copy(source, target, sem)
    copy.start()
    copy.wait()


def store(arrivals):
    return pl.pallas_call(
        store_kernel,
        out_shape=jax.ShapeDtypeStruct(arrivals.shape, F32),
        in_specs=[ANY_SPEC],
        out_specs=HBM_SPEC,
        scratch_shapes=[pltpu.SemaphoreType.DMA],
        compiler_params=pltpu.CompilerParams(vmem_limit_bytes=4 << 20),
    )(arrivals)


def per_device(
    velocity, theta_field, vapour, radius, multiplicity, solute, counts, leave_slot, leave_dir
):
    drops = (a.reshape(TILES, 8, 128) for a in (radius, multiplicity, solute))
    lists = (a.reshape(BLOCKS, 128) for a in (leave_slot, leave_dir))
    inputs = (velocity, theta_field, vapour, *drops, counts, *lists)
    *ready, values, places, stays = exchange_halo(
        *(pltpu.with_memory_space_constraint(a, pltpu.HBM) for a in inputs)
    )
    state_new, radius_new, picked, late = local_step(*ready, stays)
    arrivals = store(exchange_droplets(picked, values, places, late))
    return (state_new, radius_new.reshape(radius.shape), arrivals.reshape(3, 4, 1, 1, CAP))


def solution(mesh):
    in_specs = (
        P(None, None, "gx", "gy"),
        P(None, "gx", "gy"),
        P(None, "gx", "gy"),
        P(None, None, "gx", "gy"),
        P(None, None, "gx", "gy"),
        P(None, None, "gx", "gy"),
        P(None, "gx", "gy"),
        P("gx", "gy", None),
        P("gx", "gy", None),
    )
    out_specs = (
        P(None, None, "gx", "gy"),
        P(None, None, "gx", "gy"),
        P(None, None, "gx", "gy", None),
    )
    return jax.shard_map(
        per_device, mesh=mesh, in_specs=in_specs, out_specs=out_specs, check_vma=False
    )
```

```python
import functools

import jax
import jax.numpy as jnp
from jax import lax
from jax.experimental import pallas as pl
from jax.experimental.pallas import tpu as pltpu
from jax.sharding import PartitionSpec as P

MESH = pl.DeviceIdType.MESH
VMEM_SPEC = pl.BlockSpec(memory_space=pltpu.VMEM)
ANY_SPEC = pl.BlockSpec(memory_space=pl.ANY)
HBM_SPEC = pl.BlockSpec(memory_space=pltpu.HBM)

CX, CY, NZ, SLOTS, CAP, MIG = 16, 128, 16, 5, 2048, 8192
TILES = SLOTS * NZ * 2
BLOCKS = MIG // 128
BINS = 64
HALF = 16
GROUP = 6

TIME_STEP = 0.5
DIFFUSION = 0.05
BUOYANCY = 0.0327
SATURATION = 10.0
SAT_SLOPE = 0.06
GROWTH = 20.0
CURVATURE = 1.0
HYGROSCOPY = 1.0
FLOOR_SQUARE = 0.25
UPTAKE = 0.001
HEATING = 2.5

F32, BF16, I32 = jnp.float32, jnp.bfloat16, jnp.int32


def iota(shape, dim):
    return lax.broadcasted_iota(I32, shape, dim)


def ring(axis):
    count = lax.axis_size(axis)
    me = lax.axis_index(axis)
    return {axis: lax.rem(me + 1, count)}, {axis: lax.rem(me + count - 1, count)}


def greet(neighbours):
    for there in neighbours:
        pl.semaphore_signal(
            pltpu.get_barrier_semaphore(), inc=1, device_id=there, device_id_type=MESH
        )


def greeted(neighbours):
    pl.semaphore_wait(pltpu.get_barrier_semaphore(), len(neighbours))


def iota16(shape):
    return iota(shape, 0).astype(F32).astype(BF16)


def row16(tile, q, rows):
    return jnp.broadcast_to(tile[q : q + 1], (rows, 128)).astype(BF16)


def hot16(hit):
    return jnp.where(hit, jnp.ones(hit.shape, BF16), jnp.zeros(hit.shape, BF16))


def to_bf16(mask):
    return jnp.where(mask, 1.0, 0.0).astype(BF16)


NT = (((1,), (1,)), ((), ()))
NN = (((1,), (0,)), ((), ()))


def dot(a, b, dims=NN):
    return lax.dot_general(a, b, dims, preferred_element_type=F32)


def entry_codes(slots, ways, codes):
    before = iota((128, 128), 0) < iota((128, 128), 1)
    counter = jnp.concatenate([to_bf16(before), jnp.ones((128, 128), BF16)], 1)
    slot = slots[...]
    valid = slot >= 0
    way = jnp.where(valid, ways[...], -1)
    marks = [jnp.where(way == d, 1.0, 0.0) for d in range(4)]
    inside = dot(jnp.concatenate(marks, 0).astype(BF16), counter)
    earlier = to_bf16(iota((BLOCKS, BLOCKS), 1) < iota((BLOCKS, BLOCKS), 0))
    rank = jnp.zeros((BLOCKS, 128), F32)
    for d in range(4):
        block = inside[d * BLOCKS : (d + 1) * BLOCKS]
        offset = dot(earlier, block[:, 128:].astype(BF16))
        rank = rank + marks[d] * (block[:, :128] + offset)
    rank = rank.astype(I32)
    row = lax.shift_right_logical(slot, 7)
    inner = row & 7
    place_row = (way << 3) + (lax.shift_right_logical(rank, 7) & 7)
    column = (rank & 127) + (lax.shift_right_logical(rank, 10) << 7)
    codes[0] = jnp.where(valid, lax.shift_right_logical(row, 3) + 1, 0).astype(F32)
    codes[1] = column.astype(F32)
    codes[2] = (inner + (place_row << 3)).astype(F32)
    codes[3] = jnp.where(valid, slot & 127, -1).astype(F32)
    return counter


def spread_row(number, code8, q):
    hit = iota16((BINS, 128)) == jnp.broadcast_to(number, (BINS, 128)).astype(BF16)
    spread = []
    for n in range(3):
        value = row16(code8[n], q, BINS)
        spread.append(jnp.where(hit, value, jnp.zeros_like(value)))
    return jnp.concatenate(spread, 0)


def bin_lists(slots, ways, codes, bin_of, table, most):
    counter = entry_codes(slots, ways, codes)
    table[...] = jnp.zeros_like(table)

    def turn(t, carry):
        tile = pl.ds(pl.multiple_of(t * 8, 8), 8)
        lane8 = codes[3, tile]
        code8 = [codes[n, tile] for n in range(3)]
        found, hots, spread = [], [], []
        for q in range(8):
            hit = iota((128, 128), 0).astype(F32) == lane8[q : q + 1]
            hots.append(to_bf16(hit))
            counted = dot(hots[-1], counter)
            number = jnp.sum(
                jnp.where(hit, counted[:, :128] + carry, 0.0), axis=0, keepdims=True
            )
            carry = carry + counted[:, 128:]
            found.append(number)
            spread.append(spread_row(jnp.minimum(number, float(BINS)), code8, q))
        bin_of[tile] = jnp.concatenate(found, 0)
        table[...] += dot(jnp.concatenate(spread, 1), jnp.concatenate(hots, 1), NT)
        return carry

    most[...] = lax.fori_loop(0, BLOCKS // 8, turn, jnp.zeros((128, 128), F32), unroll=8)


PARTS = BINS // 8


def read_table(table):
    first = table[0:BINS].astype(I32)
    third = table[2 * BINS : 3 * BINS].astype(I32)
    group = first - 1
    inner = third & 7
    groups = [group[8 * m : 8 * m + 8] for m in range(PARTS)]
    inners = [inner[8 * m : 8 * m + 8] for m in range(PARTS)]
    place_row = jnp.where(first > 0, lax.shift_right_logical(third, 3), -1).astype(F32)
    return groups, inners, place_row, table[BINS : 2 * BINS]


def gather(groups, inners, sources, values, first, mark, unroll):
    bits = [jnp.left_shift(1, inners[m]) for m in range(PARTS)]
    sublane = iota((8, 128), 0)
    count = len(sources)

    def turn(j, kept):
        tiles = [source[j] for source in sources]
        kept = list(kept)
        marked = jnp.zeros((8, 128), I32)
        for m in range(PARTS):
            hit = groups[m] == j
            if mark is not None:
                marked = marked | jnp.where(hit, bits[m], 0)
            for n in range(count):
                got = jnp.take_along_axis(tiles[n], inners[m], axis=0, mode="promise_in_bounds")
                kept[n * PARTS + m] = jnp.where(hit, got, kept[n * PARTS + m])
        if mark is not None:
            marked = marked | pltpu.roll(marked, 4, 0)
            marked = marked | pltpu.roll(marked, 2, 0)
            marked = marked | pltpu.roll(marked, 1, 0)
            mark(j, (lax.shift_right_logical(marked, sublane) & 1) == 1)
        return tuple(kept)

    start = tuple(jnp.zeros((8, 128), F32) for _ in range(count * PARTS))
    kept = lax.fori_loop(0, TILES, turn, start, unroll=unroll)
    for n in range(count):
        for m in range(PARTS):
            values[first + n, 8 * m : 8 * m + 8] = kept[n * PARTS + m]


def place_bins(tile_of, places, out_acc, unroll):
    def turn(t, _):
        tile = pl.ds(pl.multiple_of(t * 8, 8), 8)
        row8, column8 = places[0, tile], places[1, tile]
        whole = tile_of(tile)
        high = [value.astype(BF16).astype(F32) for value in whole]
        low = [value - part for value, part in zip(whole, high)]
        rows, columns = [], []
        for q in range(8):
            hit = iota16((2 * HALF, 128)) == row16(row8, q, 2 * HALF)
            parts = []
            for piece in high + low:
                value = row16(piece, q, 2 * HALF)
                parts.append(jnp.where(hit, value, jnp.zeros_like(value)))
            rows.append(jnp.concatenate(parts, 0))
            columns.append(hot16(iota16((256, 128)) == row16(column8, q, 256)))
        out_acc[...] += dot(jnp.concatenate(rows, 1), jnp.concatenate(columns, 1), NT)
        return _

    lax.fori_loop(0, PARTS, turn, 0, unroll=unroll)


def halo_kernel(
    vel, theta, vap, radius_in, mult_in, sol_in, counts_in, slots_in, ways_in,
    pad, yhalo, radius, mult, sol, counts, codes, bin_of, table, most, weights, values, places, stays,
    packed, landed, slots, ways, local_sem, send_sem, recv_sem,
):
    east, west = ring("gx")
    north, south = ring("gy")
    neighbours = (east, west, north, south)
    greet(neighbours)
    pairs = (
        (vel, pad.at[0:3, :, 8:24, :]),
        (theta, pad.at[3, :, 8:24, :]),
        (vap, pad.at[4, :, 8:24, :]),
        (slots_in, slots),
        (ways_in, ways),
        (radius_in, radius),
        (mult_in, mult),
        (sol_in, sol),
        (counts_in, counts),
    )
    loads = [
        pltpu.make_async_copy(source, target, local_sem.at[number])
        for number, (source, target) in enumerate(pairs)
    ]
    for copy in loads:
        copy.start()
    for copy in loads[:3]:
        copy.wait()

    turned = lax.rem(iota((16, 128), 1) + 3, 128)
    number = turned // GROUP

    def pack(quarter, _):
        total = jnp.zeros((16, 128), F32)
        for inner_level in range(4):
            for f in range(5):
                g = inner_level * 5 + f
                value = pad[f, quarter * 4 + inner_level, 8:24]
                if g:
                    value = pltpu.roll(value, GROUP * g, 1)
                total = jnp.where(number == g, value, total)
        packed[quarter] = total
        return _

    lax.fori_loop(0, 4, pack, 0)
    greeted(neighbours)
    routes = (
        (packed, landed.at[0], north),
        (packed, landed.at[1], south),
        (pad.at[:, :, 21:24, :], pad.at[:, :, 5:8, :], east),
        (pad.at[:, :, 8:11, :], pad.at[:, :, 24:27, :], west),
    )
    sends = [
        pltpu.make_async_remote_copy(
            src_ref=source,
            dst_ref=target,
            send_sem=send_sem.at[number],
            recv_sem=recv_sem.at[number],
            device_id=there,
            device_id_type=MESH,
        )
        for number, (source, target, there) in enumerate(routes)
    ]
    for copy in sends:
        copy.start()
    for copy in loads[3:5]:
        copy.wait()
    weights[...] = line_weights()
    bin_lists(slots, ways, codes, bin_of, table, most)
    for copy in loads[5:]:
        copy.wait()
    groups, inners, places[0], places[1] = read_table(table)

    def mark(j, left):
        stays[j] = jnp.where(left, 0.0, 1.0)

    gather(groups, inners, (mult, sol), values, 0, mark, 8)
    sends[0].wait_recv()
    sends[1].wait_recv()
    from_south = turned - number * GROUP < 3
    for quarter in range(4):
        yhalo[quarter] = jnp.where(from_south, landed[0, quarter], landed[1, quarter])
    sends[2].wait_recv()
    sends[3].wait_recv()
    for copy in sends:
        copy.wait_send()


def exchange_halo(velocity, theta_field, vapour, radius, multiplicity, solute, counts, slots, ways):
    drops = jax.ShapeDtypeStruct((TILES, 8, 128), F32)
    return pl.pallas_call(
        halo_kernel,
        out_shape=(
            jax.ShapeDtypeStruct((5, NZ, 32, CY), F32),
            jax.ShapeDtypeStruct((4, 16, 128), F32),
            drops,
            drops,
            drops,
            jax.ShapeDtypeStruct((NZ, CX, CY), I32),
            jax.ShapeDtypeStruct((4, BLOCKS, 128), F32),
            jax.ShapeDtypeStruct((BLOCKS, 128), F32),
            jax.ShapeDtypeStruct((3 * BINS, 128), F32),
            jax.ShapeDtypeStruct((128, 128), F32),
            jax.ShapeDtypeStruct((512, 384), BF16),
            jax.ShapeDtypeStruct((2, BINS, 128), F32),
            jax.ShapeDtypeStruct((2, BINS, 128), F32),
            drops,
        ),
        in_specs=[HBM_SPEC] * 9,
        out_specs=(VMEM_SPEC,) * 14,
        scratch_shapes=[
            pltpu.VMEM((4, 16, 128), F32),
            pltpu.VMEM((2, 4, 16, 128), F32),
            pltpu.VMEM((BLOCKS, 128), I32),
            pltpu.VMEM((BLOCKS, 128), I32),
            pltpu.SemaphoreType.DMA((9,)),
            pltpu.SemaphoreType.DMA((4,)),
            pltpu.SemaphoreType.DMA((4,)),
        ],
        compiler_params=pltpu.CompilerParams(
            collective_id=0, has_side_effects=True, vmem_limit_bytes=24 << 20
        ),
    )(velocity, theta_field, vapour, radius, multiplicity, solute, counts, slots, ways)


def line_weights():
    apart = iota((128, 128), 0) - iota((128, 128), 1)

    def weights(far):
        size = jnp.abs(far)
        sign = jnp.where(far < 0, -1.0, 1.0)
        centred = jnp.where(size == 1, 45.0, jnp.where(size == 2, -9.0, jnp.where(size == 3, 1.0, 0.0)))
        damping = jnp.where(
            size == 0, -20.0,
            jnp.where(size == 1, 15.0, jnp.where(size == 2, -6.0, jnp.where(size == 3, 1.0, 0.0))),
        )
        beside = jnp.where(size == 1, 1.0, 0.0)
        return jnp.concatenate([centred * sign, damping, beside], 1)

    own = weights(apart)
    halo = weights(apart + 128) + weights(apart - 128)
    return jnp.concatenate([own, own, halo, halo], 0).astype(BF16)


def line_sums(quarter, fields, pad, yhalo, weights, lines, along):
    for inner_level in range(4):
        for position, f in enumerate(fields):
            g = inner_level * 5 + f
            edge = yhalo[quarter]
            if g:
                edge = pltpu.roll(edge, 128 - GROUP * g, 1)
            first = 16 * (inner_level * len(fields) + position)
            for part, value in enumerate((pad[f, quarter * 4 + inner_level, 8:24], edge)):
                high = value.astype(BF16)
                low = (value - high.astype(F32)).astype(BF16)
                lines[quarter, first : first + 16, 256 * part : 256 * part + 128] = high
                lines[quarter, first : first + 16, 256 * part + 128 : 256 * part + 256] = low
    along[quarter] = dot(lines[quarter], weights[...])


def advance(quarter, inner_level, half, fields, pad, along):
    k = quarter * 4 + inner_level
    above, below = min(k + 1, NZ - 1), max(k - 1, 0)
    base = 8 + 8 * half
    u = pad[0, k, base : base + 8] * (-TIME_STEP / 60.0)
    v = pad[1, k, base : base + 8] * (-TIME_STEP / 60.0)
    w = pad[2, k, base : base + 8]
    lift = DIFFUSION * TIME_STEP - w * (0.5 * TIME_STEP)
    sink = DIFFUSION * TIME_STEP + w * (0.5 * TIME_STEP)
    u_size, v_size = jnp.abs(u), jnp.abs(v)
    moved = []
    for position, f in enumerate(fields):
        mid = pad[f, k, base : base + 8]
        p1, m1, p2, m2, p3, m3 = (
            pad[f, k, base + d : base + d + 8] for d in (1, -1, 2, -2, 3, -3)
        )
        first = 16 * (inner_level * len(fields) + position) + 8 * half
        y_centred, y_damping, y_beside = (
            along[quarter, first : first + 8, 128 * n : 128 * n + 128] for n in range(3)
        )
        s1 = p1 + m1
        total = mid + u * (45.0 * (p1 - m1) - 9.0 * (p2 - m2) + (p3 - m3))
        total = total + u_size * (15.0 * s1 - 6.0 * (p2 + m2) + (p3 + m3) - 20.0 * mid)
        total = total + v * y_centred + v_size * y_damping
        total = total + (DIFFUSION * TIME_STEP) * (s1 + y_beside - 6.0 * mid)
        total = total + lift * pad[f, above, base : base + 8] + sink * pad[f, below, base : base + 8]
        if f == 2:
            total = total + (TIME_STEP * BUOYANCY) * pad[3, k, base : base + 8]
        moved.append(total)
    return moved


def staged(first_step, second_step):
    first_step(0)
    for quarter in range(4):
        if quarter < 3:
            first_step(quarter + 1)
        second_step(quarter)


def grow(pad, yhalo, radius, sol, counts, stays, weights, heat, rnew, grown, lines, along):
    fields = (3, 4)

    def sums(quarter):
        line_sums(quarter, fields, pad, yhalo, weights, lines, along)

    def cells(quarter):
        for inner_level in range(4):
            k = quarter * 4 + inner_level
            for half in range(2):
                rows = slice(8 * half, 8 * half + 8)
                theta, vapour = advance(quarter, inner_level, half, fields, pad, along)
                heat[0, k, rows] = theta
                heat[1, k, rows] = vapour
                supersat = vapour * (jnp.exp(-SAT_SLOPE * theta) * (1.0 / SATURATION)) - 1.0
                alive_count = counts[k, rows]
                for s in range(SLOTS):
                    tile = (s * NZ + k) * 2 + half
                    r = radius[tile]
                    inv = 1.0 / r
                    square = r * r + GROWTH * (
                        supersat - CURVATURE * inv + (HYGROSCOPY * sol[tile]) * (inv * inv * inv)
                    )
                    new = jnp.sqrt(jnp.maximum(square, FLOOR_SQUARE))
                    grown[tile] = new
                    rnew[tile] = jnp.where(s < alive_count, new * stays[tile], 0.0)

    staged(sums, cells)


def finish_state(pad, yhalo, radius, mult, counts, grown, heat, weights, state, lines, along):
    fields = (0, 1, 2)

    def sums(quarter):
        line_sums(quarter, fields, pad, yhalo, weights, lines, along)

    def cells(quarter):
        for inner_level in range(4):
            k = quarter * 4 + inner_level
            for half in range(2):
                rows = slice(8 * half, 8 * half + 8)
                for f, value in enumerate(advance(quarter, inner_level, half, fields, pad, along)):
                    state[f, k, rows] = value
                alive_count = counts[k, rows]
                condensed = jnp.zeros((8, 128), F32)
                for s in range(SLOTS):
                    tile = (s * NZ + k) * 2 + half
                    r, new = radius[tile], grown[tile]
                    condensed = condensed + jnp.where(
                        s < alive_count, mult[tile] * (new * new * new - r * r * r), 0.0
                    )
                state[3, k, rows] = heat[0, k, rows] + (HEATING * UPTAKE) * condensed
                state[4, k, rows] = heat[1, k, rows] - UPTAKE * condensed

    staged(sums, cells)


def late_turn(chunk, codes, bin_of, table, values, places, grown, mult, sol, rnew, out_acc):
    table[...] = jnp.zeros_like(table)

    def spread_turn(t, _):
        tile = pl.ds(pl.multiple_of(t * 8, 8), 8)
        first = (chunk * BINS).astype(F32)
        bins8 = jnp.maximum(jnp.minimum(bin_of[tile] - first, float(BINS)), -1.0)
        lane8 = codes[3, tile]
        code8 = [codes[n, tile] for n in range(3)]
        hots = [to_bf16(iota((128, 128), 0).astype(F32) == lane8[q : q + 1]) for q in range(8)]
        spread = [spread_row(bins8[q : q + 1], code8, q) for q in range(8)]
        table[...] += dot(jnp.concatenate(spread, 1), jnp.concatenate(hots, 1), NT)
        return _

    lax.fori_loop(0, BLOCKS // 8, spread_turn, 0)
    groups, inners, places[0], places[1] = read_table(table)

    def mark(j, left):
        rnew[j] = jnp.where(left, 0.0, rnew[j])

    gather(groups, inners, (grown, mult, sol), values, 0, mark, 1)
    place_bins(lambda tile: [values[n, tile] for n in range(3)], places, out_acc, 1)


def local_kernel(
    pad, yhalo, radius, mult, sol, counts, codes, bin_of, table, most, weights, stays,
    rnew_out, picked, late, grown, heat,
    rnew, lines, along, late_table, values, places, sem,
):
    chunks = (jnp.max(most[...]).astype(I32) + BINS - 1) // BINS
    late[...] = jnp.zeros_like(late)
    grow(pad, yhalo, radius, sol, counts, stays, weights, heat, rnew, grown, lines, along)

    def turn(chunk, _):
        late_turn(chunk, codes, bin_of, late_table, values, places, grown, mult, sol, rnew, late)
        return _

    lax.fori_loop(1, chunks, turn, 0)
    save = pltpu.make_async_copy(rnew, rnew_out, sem)
    save.start()
    groups, inners, _, _ = read_table(table)
    gather(groups, inners, (grown,), picked, 0, None, 16)
    save.wait()


def local_step(*operands):
    return pl.pallas_call(
        local_kernel,
        out_shape=(
            jax.ShapeDtypeStruct((TILES, 8, 128), F32),
            jax.ShapeDtypeStruct((1, BINS, 128), F32),
            jax.ShapeDtypeStruct((12 * HALF, 256), F32),
            jax.ShapeDtypeStruct((TILES, 8, 128), F32),
            jax.ShapeDtypeStruct((2, NZ, CX, CY), F32),
        ),
        in_specs=[VMEM_SPEC] * 12,
        out_specs=(HBM_SPEC,) + (VMEM_SPEC,) * 4,
        scratch_shapes=[
            pltpu.VMEM((TILES, 8, 128), F32),
            pltpu.VMEM((4, 128, 512), BF16),
            pltpu.VMEM((4, 128, 384), F32),
            pltpu.VMEM((3 * BINS, 128), F32),
            pltpu.VMEM((3, BINS, 128), F32),
            pltpu.VMEM((2, BINS, 128), F32),
            pltpu.SemaphoreType.DMA,
        ],
        compiler_params=pltpu.CompilerParams(vmem_limit_bytes=24 << 20),
    )(*operands)


def droplet_kernel(
    picked, values, places, late, pad, yhalo, radius, mult, counts, grown, heat, weights,
    arrivals, state,
    out_acc, outgoing, lines, along, send_sem, recv_sem,
):
    east, west = ring("gx")
    north, south = ring("gy")
    ways = (east, west, north, south)
    greet(ways)
    out_acc[...] = late[...]
    place_bins(lambda tile: [picked[0, tile], values[0, tile], values[1, tile]], places, out_acc, PARTS)
    for d in range(4):
        for n in range(3):
            first = n * 2 * HALF + d * 8
            total = out_acc[first : first + 8] + out_acc[first + 6 * HALF : first + 6 * HALF + 8]
            outgoing[d, n, 0:8] = total[:, :128]
            outgoing[d, n, 8:16] = total[:, 128:]
    greeted(ways)
    sends = [
        pltpu.make_async_remote_copy(
            src_ref=outgoing.at[d],
            dst_ref=arrivals.at[:, d],
            send_sem=send_sem.at[d],
            recv_sem=recv_sem.at[d],
            device_id=there,
            device_id_type=MESH,
        )
        for d, there in enumerate(ways)
    ]
    for copy in sends:
        copy.start()
    finish_state(pad, yhalo, radius, mult, counts, grown, heat, weights, state, lines, along)
    for copy in sends:
        copy.wait()


def exchange_droplets(*operands):
    return pl.pallas_call(
        droplet_kernel,
        out_shape=(
            jax.ShapeDtypeStruct((3, 4, CAP // 128, 128), F32),
            jax.ShapeDtypeStruct((5, NZ, CX, CY), F32),
        ),
        in_specs=[VMEM_SPEC] * 12,
        out_specs=(ANY_SPEC, VMEM_SPEC),
        scratch_shapes=[
            pltpu.VMEM((12 * HALF, 256), F32),
            pltpu.VMEM((4, 3, CAP // 128, 128), F32),
            pltpu.VMEM((4, 192, 512), BF16),
            pltpu.VMEM((4, 192, 384), F32),
            pltpu.SemaphoreType.DMA((4,)),
            pltpu.SemaphoreType.DMA((4,)),
        ],
        compiler_params=pltpu.CompilerParams(
            collective_id=1, has_side_effects=True, vmem_limit_bytes=16 << 20
        ),
    )(*operands)


def store_kernel(arrivals, state, arrivals_out, state_out, sems):
    copies = (
        pltpu.make_async_copy(state, state_out, sems.at[0]),
        pltpu.make_async_copy(arrivals, arrivals_out, sems.at[1]),
    )
    for copy in copies:
        copy.start()
    for copy in copies:
        copy.wait()


def store(arrivals, state):
    return pl.pallas_call(
        store_kernel,
        out_shape=(
            jax.ShapeDtypeStruct(arrivals.shape, F32),
            jax.ShapeDtypeStruct(state.shape, F32),
        ),
        in_specs=[ANY_SPEC] * 2,
        out_specs=(HBM_SPEC,) * 2,
        scratch_shapes=[pltpu.SemaphoreType.DMA((2,))],
        compiler_params=pltpu.CompilerParams(vmem_limit_bytes=4 << 20),
    )(arrivals, state)


def per_device(
    velocity, theta_field, vapour, radius, multiplicity, solute, counts, leave_slot, leave_dir
):
    drops = (a.reshape(TILES, 8, 128) for a in (radius, multiplicity, solute))
    lists = (a.reshape(BLOCKS, 128) for a in (leave_slot, leave_dir))
    inputs = (velocity, theta_field, vapour, *drops, counts, *lists)
    *ready, values, places, stays = exchange_halo(
        *(pltpu.with_memory_space_constraint(a, pltpu.HBM) for a in inputs)
    )
    pad, yhalo, radii, mult, _, alive, *_, weights = ready
    radius_new, picked, late, grown, heat = local_step(*ready, stays)
    arrivals, state_new = store(
        *exchange_droplets(
            picked, values, places, late, pad, yhalo, radii, mult, alive, grown, heat, weights
        )
    )
    return (state_new, radius_new.reshape(radius.shape), arrivals.reshape(3, 4, 1, 1, CAP))


def solution(mesh):
    in_specs = (
        P(None, None, "gx", "gy"),
        P(None, "gx", "gy"),
        P(None, "gx", "gy"),
        P(None, None, "gx", "gy"),
        P(None, None, "gx", "gy"),
        P(None, None, "gx", "gy"),
        P(None, "gx", "gy"),
        P("gx", "gy", None),
        P("gx", "gy", None),
    )
    out_specs = (
        P(None, None, "gx", "gy"),
        P(None, None, "gx", "gy"),
        P(None, None, "gx", "gy", None),
    )
    return jax.shard_map(
        per_device, mesh=mesh, in_specs=in_specs, out_specs=out_specs, check_vma=False
    )
```

```python
import functools

import jax
import jax.numpy as jnp
from jax import lax
from jax.experimental import pallas as pl
from jax.experimental.pallas import tpu as pltpu
from jax.sharding import PartitionSpec as P

MESH = pl.DeviceIdType.MESH
VMEM_SPEC = pl.BlockSpec(memory_space=pltpu.VMEM)
ANY_SPEC = pl.BlockSpec(memory_space=pl.ANY)
HBM_SPEC = pl.BlockSpec(memory_space=pltpu.HBM)

CX, CY, NZ, SLOTS, CAP, MIG = 16, 128, 16, 5, 2048, 8192
TILES = SLOTS * NZ * 2
CELLS = NZ * 2
BLOCKS = MIG // 128
BINS = 64
HALF = 16
GROUP = 6

TIME_STEP = 0.5
DIFFUSION = 0.05
BUOYANCY = 0.0327
SATURATION = 10.0
SAT_SLOPE = 0.06
GROWTH = 20.0
CURVATURE = 1.0
HYGROSCOPY = 1.0
FLOOR_SQUARE = 0.25
UPTAKE = 0.001
HEATING = 2.5

F32, BF16, I32 = jnp.float32, jnp.bfloat16, jnp.int32


def iota(shape, dim):
    return lax.broadcasted_iota(I32, shape, dim)


def ring(axis):
    count = lax.axis_size(axis)
    me = lax.axis_index(axis)
    return {axis: lax.rem(me + 1, count)}, {axis: lax.rem(me + count - 1, count)}


def greet(neighbours):
    for there in neighbours:
        pl.semaphore_signal(
            pltpu.get_barrier_semaphore(), inc=1, device_id=there, device_id_type=MESH
        )


def greeted(neighbours):
    pl.semaphore_wait(pltpu.get_barrier_semaphore(), len(neighbours))


def iota16(shape):
    return iota(shape, 0).astype(F32).astype(BF16)


def row16(tile, q, rows):
    return jnp.broadcast_to(tile[q : q + 1], (rows, 128)).astype(BF16)


def hot16(hit):
    return jnp.where(hit, jnp.ones(hit.shape, BF16), jnp.zeros(hit.shape, BF16))


def to_bf16(mask):
    return jnp.where(mask, 1.0, 0.0).astype(BF16)


NT = (((1,), (1,)), ((), ()))
NN = (((1,), (0,)), ((), ()))


def dot(a, b, dims=NN):
    return lax.dot_general(a, b, dims, preferred_element_type=F32)


def entry_codes(slots, ways, codes):
    before = iota((128, 128), 0) < iota((128, 128), 1)
    counter = jnp.concatenate([to_bf16(before), jnp.ones((128, 128), BF16)], 1)
    slot = slots[...]
    valid = slot >= 0
    way = jnp.where(valid, ways[...], -1)
    marks = [jnp.where(way == d, 1.0, 0.0) for d in range(4)]
    inside = dot(jnp.concatenate(marks, 0).astype(BF16), counter)
    earlier = to_bf16(iota((BLOCKS, BLOCKS), 1) < iota((BLOCKS, BLOCKS), 0))
    rank = jnp.zeros((BLOCKS, 128), F32)
    for d in range(4):
        block = inside[d * BLOCKS : (d + 1) * BLOCKS]
        offset = dot(earlier, block[:, 128:].astype(BF16))
        rank = rank + marks[d] * (block[:, :128] + offset)
    rank = rank.astype(I32)
    row = lax.shift_right_logical(slot, 7)
    inner = row & 7
    place_row = (way << 3) + (lax.shift_right_logical(rank, 7) & 7)
    column = (rank & 127) + (lax.shift_right_logical(rank, 10) << 7)
    codes[0] = jnp.where(valid, lax.shift_right_logical(row, 3) + 1, 0).astype(F32)
    codes[1] = column.astype(F32)
    codes[2] = (inner + (place_row << 3)).astype(F32)
    codes[3] = jnp.where(valid, slot & 127, -1).astype(F32)
    return counter


def spread_row(number, code8, q):
    hit = iota16((BINS, 128)) == jnp.broadcast_to(number, (BINS, 128)).astype(BF16)
    spread = []
    for n in range(3):
        value = row16(code8[n], q, BINS)
        spread.append(jnp.where(hit, value, jnp.zeros_like(value)))
    return jnp.concatenate(spread, 0)


def bin_lists(counter, codes, bin_of, table, most):
    table[...] = jnp.zeros_like(table)

    def turn(t, carry):
        tile = pl.ds(pl.multiple_of(t * 8, 8), 8)
        lane8 = codes[3, tile]
        code8 = [codes[n, tile] for n in range(3)]
        found, hots, spread = [], [], []
        for q in range(8):
            hit = iota((128, 128), 0).astype(F32) == lane8[q : q + 1]
            hots.append(to_bf16(hit))
            counted = dot(hots[-1], counter)
            number = jnp.sum(
                jnp.where(hit, counted[:, :128] + carry, 0.0), axis=0, keepdims=True
            )
            carry = carry + counted[:, 128:]
            found.append(number)
            spread.append(spread_row(jnp.minimum(number, float(BINS)), code8, q))
        bin_of[tile] = jnp.concatenate(found, 0)
        table[...] += dot(jnp.concatenate(spread, 1), jnp.concatenate(hots, 1), NT)
        return carry

    most[...] = lax.fori_loop(0, BLOCKS // 8, turn, jnp.zeros((128, 128), F32), unroll=8)


PARTS = BINS // 8


def read_table(table):
    first = table[0:BINS].astype(I32)
    third = table[2 * BINS : 3 * BINS].astype(I32)
    group = first - 1
    inner = third & 7
    groups = [group[8 * m : 8 * m + 8] for m in range(PARTS)]
    inners = [inner[8 * m : 8 * m + 8] for m in range(PARTS)]
    place_row = jnp.where(first > 0, lax.shift_right_logical(third, 3), -1).astype(F32)
    return groups, inners, place_row, table[BINS : 2 * BINS]


def gather(groups, inners, sources, values, unroll):
    count = len(sources)

    def turn(j, kept):
        tiles = [source[j] for source in sources]
        kept = list(kept)
        for m in range(PARTS):
            hit = groups[m] == j
            for n in range(count):
                got = jnp.take_along_axis(tiles[n], inners[m], axis=0, mode="promise_in_bounds")
                kept[n * PARTS + m] = jnp.where(hit, got, kept[n * PARTS + m])
        return tuple(kept)

    start = tuple(jnp.zeros((8, 128), F32) for _ in range(count * PARTS))
    kept = lax.fori_loop(0, sources[0].shape[0], turn, start, unroll=unroll)
    for n in range(count):
        for m in range(PARTS):
            values[n, 8 * m : 8 * m + 8] = kept[n * PARTS + m]


def clear_left(groups, inners, slots, unroll):
    bits = [jnp.left_shift(1, inners[m]) for m in range(PARTS)]
    sublane = iota((8, 128), 0)

    def turn(j, _):
        marked = jnp.zeros((8, 128), I32)
        for m in range(PARTS):
            marked = marked | jnp.where(groups[m] == j, bits[m], 0)
        marked = marked | pltpu.roll(marked, 4, 0)
        marked = marked | pltpu.roll(marked, 2, 0)
        marked = marked | pltpu.roll(marked, 1, 0)
        left = (lax.shift_right_logical(marked, sublane) & 1) == 1
        slots[j] = jnp.where(left, 0.0, slots[j])
        return _

    lax.fori_loop(0, TILES, turn, 0, unroll=unroll)


def new_radius(r, solute, supersat):
    inv = 1.0 / r
    square = r * r + GROWTH * (
        supersat - CURVATURE * inv + (HYGROSCOPY * solute) * (inv * inv * inv)
    )
    return jnp.sqrt(jnp.maximum(square, FLOOR_SQUARE))


def grow_bins(groups, inners, supersat, wet, values, picked, unroll):
    gather([group & (CELLS - 1) for group in groups], inners, (supersat,), wet, unroll)
    for m in range(PARTS):
        rows = slice(8 * m, 8 * m + 8)
        r = jnp.where(groups[m] < 0, 1.0, values[0, rows])
        picked[rows] = new_radius(r, values[2, rows], wet[0, rows])


def place_bins(tile_of, places, out_acc, unroll):
    def turn(t, _):
        tile = pl.ds(pl.multiple_of(t * 8, 8), 8)
        row8, column8 = places[0, tile], places[1, tile]
        whole = tile_of(tile)
        high = [value.astype(BF16).astype(F32) for value in whole]
        low = [value - part for value, part in zip(whole, high)]
        rows, columns = [], []
        for q in range(8):
            hit = iota16((2 * HALF, 128)) == row16(row8, q, 2 * HALF)
            parts = []
            for piece in high + low:
                value = row16(piece, q, 2 * HALF)
                parts.append(jnp.where(hit, value, jnp.zeros_like(value)))
            rows.append(jnp.concatenate(parts, 0))
            columns.append(hot16(iota16((256, 128)) == row16(column8, q, 256)))
        out_acc[...] += dot(jnp.concatenate(rows, 1), jnp.concatenate(columns, 1), NT)
        return _

    lax.fori_loop(0, PARTS, turn, 0, unroll=unroll)


def halo_kernel(
    vel, theta, vap, radius_in, mult_in, sol_in, counts_in, slots_in, ways_in,
    pad, yhalo, radius, mult, sol, counts, codes, bin_of, table, most, weights, values, places,
    packed, landed, slots, ways, local_sem, send_sem, recv_sem,
):
    east, west = ring("gx")
    north, south = ring("gy")
    neighbours = (east, west, north, south)
    greet(neighbours)
    pairs = (
        (slots_in, slots),
        (ways_in, ways),
        (vel, pad.at[0:3, :, 8:24, :]),
        (theta, pad.at[3, :, 8:24, :]),
        (vap, pad.at[4, :, 8:24, :]),
        (radius_in, radius),
        (mult_in, mult),
        (sol_in, sol),
        (counts_in, counts),
    )
    loads = [
        pltpu.make_async_copy(source, target, local_sem.at[number])
        for number, (source, target) in enumerate(pairs)
    ]
    for copy in loads:
        copy.start()
    weights[...] = line_weights()
    for copy in loads[2:5]:
        copy.wait()

    turned = lax.rem(iota((16, 128), 1) + 3, 128)
    number = turned // GROUP

    def pack(quarter, _):
        total = jnp.zeros((16, 128), F32)
        for inner_level in range(4):
            for f in range(5):
                g = inner_level * 5 + f
                value = pad[f, quarter * 4 + inner_level, 8:24]
                if g:
                    value = pltpu.roll(value, GROUP * g, 1)
                total = jnp.where(number == g, value, total)
        packed[quarter] = total
        return _

    routes = (
        (pad.at[:, :, 21:24, :], pad.at[:, :, 5:8, :], east),
        (pad.at[:, :, 8:11, :], pad.at[:, :, 24:27, :], west),
        (packed, landed.at[0], north),
        (packed, landed.at[1], south),
    )
    sends = [
        pltpu.make_async_remote_copy(
            src_ref=source,
            dst_ref=target,
            send_sem=send_sem.at[number],
            recv_sem=recv_sem.at[number],
            device_id=there,
            device_id_type=MESH,
        )
        for number, (source, target, there) in enumerate(routes)
    ]
    lax.fori_loop(0, 4, pack, 0, unroll=4)
    greeted(neighbours)
    for copy in sends:
        copy.start()
    for copy in loads[:2]:
        copy.wait()
    bin_lists(entry_codes(slots, ways, codes), codes, bin_of, table, most)
    for copy in loads[5:]:
        copy.wait()
    groups, inners, places[0], places[1] = read_table(table)
    gather(groups, inners, (radius, mult, sol), values, 8)
    sends[2].wait_recv()
    sends[3].wait_recv()
    from_south = turned - number * GROUP < 3
    for quarter in range(4):
        yhalo[quarter] = jnp.where(from_south, landed[0, quarter], landed[1, quarter])
    sends[0].wait_recv()
    sends[1].wait_recv()
    for copy in sends:
        copy.wait_send()


def exchange_halo(velocity, theta_field, vapour, radius, multiplicity, solute, counts, slots, ways):
    drops = jax.ShapeDtypeStruct((TILES, 8, 128), F32)
    return pl.pallas_call(
        halo_kernel,
        out_shape=(
            jax.ShapeDtypeStruct((5, NZ, 32, CY), F32),
            jax.ShapeDtypeStruct((4, 16, 128), F32),
            drops,
            drops,
            drops,
            jax.ShapeDtypeStruct((NZ, CX, CY), I32),
            jax.ShapeDtypeStruct((4, BLOCKS, 128), F32),
            jax.ShapeDtypeStruct((BLOCKS, 128), F32),
            jax.ShapeDtypeStruct((3 * BINS, 128), F32),
            jax.ShapeDtypeStruct((128, 128), F32),
            jax.ShapeDtypeStruct((512, 384), BF16),
            jax.ShapeDtypeStruct((3, BINS, 128), F32),
            jax.ShapeDtypeStruct((2, BINS, 128), F32),
        ),
        in_specs=[HBM_SPEC] * 9,
        out_specs=(VMEM_SPEC,) * 13,
        scratch_shapes=[
            pltpu.VMEM((4, 16, 128), F32),
            pltpu.VMEM((2, 4, 16, 128), F32),
            pltpu.VMEM((BLOCKS, 128), I32),
            pltpu.VMEM((BLOCKS, 128), I32),
            pltpu.SemaphoreType.DMA((9,)),
            pltpu.SemaphoreType.DMA((4,)),
            pltpu.SemaphoreType.DMA((4,)),
        ],
        compiler_params=pltpu.CompilerParams(
            collective_id=0, has_side_effects=True, vmem_limit_bytes=24 << 20
        ),
    )(velocity, theta_field, vapour, radius, multiplicity, solute, counts, slots, ways)


def line_weights():
    apart = iota((128, 128), 0) - iota((128, 128), 1)

    def weights(far):
        size = jnp.abs(far)
        sign = jnp.where(far < 0, -1.0, 1.0)
        centred = jnp.where(size == 1, 45.0, jnp.where(size == 2, -9.0, jnp.where(size == 3, 1.0, 0.0)))
        damping = jnp.where(
            size == 0, -20.0,
            jnp.where(size == 1, 15.0, jnp.where(size == 2, -6.0, jnp.where(size == 3, 1.0, 0.0))),
        )
        beside = jnp.where(size == 1, 1.0, 0.0)
        return jnp.concatenate([centred * sign, damping, beside], 1)

    own = weights(apart)
    halo = weights(apart + 128) + weights(apart - 128)
    return jnp.concatenate([own, own, halo, halo], 0).astype(BF16)


def line_sums(quarter, fields, pad, yhalo, weights, lines, along):
    for inner_level in range(4):
        for position, f in enumerate(fields):
            g = inner_level * 5 + f
            edge = yhalo[quarter]
            if g:
                edge = pltpu.roll(edge, 128 - GROUP * g, 1)
            first = 16 * (inner_level * len(fields) + position)
            for part, value in enumerate((pad[f, quarter * 4 + inner_level, 8:24], edge)):
                high = value.astype(BF16)
                low = (value - high.astype(F32)).astype(BF16)
                lines[quarter, first : first + 16, 256 * part : 256 * part + 128] = high
                lines[quarter, first : first + 16, 256 * part + 128 : 256 * part + 256] = low
    along[quarter] = dot(lines[quarter], weights[...])


def advance(quarter, inner_level, half, fields, pad, along):
    k = quarter * 4 + inner_level
    above, below = min(k + 1, NZ - 1), max(k - 1, 0)
    base = 8 + 8 * half
    u = pad[0, k, base : base + 8] * (-TIME_STEP / 60.0)
    v = pad[1, k, base : base + 8] * (-TIME_STEP / 60.0)
    w = pad[2, k, base : base + 8]
    lift = DIFFUSION * TIME_STEP - w * (0.5 * TIME_STEP)
    sink = DIFFUSION * TIME_STEP + w * (0.5 * TIME_STEP)
    u_size, v_size = jnp.abs(u), jnp.abs(v)
    moved = []
    for position, f in enumerate(fields):
        mid = pad[f, k, base : base + 8]
        p1, m1, p2, m2, p3, m3 = (
            pad[f, k, base + d : base + d + 8] for d in (1, -1, 2, -2, 3, -3)
        )
        first = 16 * (inner_level * len(fields) + position) + 8 * half
        y_centred, y_damping, y_beside = (
            along[quarter, first : first + 8, 128 * n : 128 * n + 128] for n in range(3)
        )
        s1 = p1 + m1
        total = mid + u * (45.0 * (p1 - m1) - 9.0 * (p2 - m2) + (p3 - m3))
        total = total + u_size * (15.0 * s1 - 6.0 * (p2 + m2) + (p3 + m3) - 20.0 * mid)
        total = total + v * y_centred + v_size * y_damping
        total = total + (DIFFUSION * TIME_STEP) * (s1 + y_beside - 6.0 * mid)
        total = total + lift * pad[f, above, base : base + 8] + sink * pad[f, below, base : base + 8]
        if f == 2:
            total = total + (TIME_STEP * BUOYANCY) * pad[3, k, base : base + 8]
        moved.append(total)
    return moved


def staged(first_step, second_step):
    first_step(0)
    for quarter in range(4):
        if quarter < 3:
            first_step(quarter + 1)
        second_step(quarter)


def moisten(pad, yhalo, weights, heat, supersat, lines, along):
    fields = (3, 4)

    def sums(quarter):
        line_sums(quarter, fields, pad, yhalo, weights, lines, along)

    def cells(quarter):
        for inner_level in range(4):
            for half in range(2):
                tile = (quarter * 4 + inner_level) * 2 + half
                theta, vapour = advance(quarter, inner_level, half, fields, pad, along)
                heat[0, tile] = theta
                heat[1, tile] = vapour
                supersat[tile] = vapour * (jnp.exp(-SAT_SLOPE * theta) * (1.0 / SATURATION)) - 1.0

    staged(sums, cells)


def finish(
    pad, yhalo, radius, mult, sol, counts, stays, heat, supersat, weights, state, rnew, lines, along
):
    fields = (0, 1, 2)

    def sums(quarter):
        line_sums(quarter, fields, pad, yhalo, weights, lines, along)

    def cells(quarter):
        for inner_level in range(4):
            k = quarter * 4 + inner_level
            for half in range(2):
                rows = slice(8 * half, 8 * half + 8)
                cell = k * 2 + half
                for f, value in enumerate(advance(quarter, inner_level, half, fields, pad, along)):
                    state[f, k, rows] = value
                alive_count, wet = counts[k, rows], supersat[cell]
                condensed = jnp.zeros((8, 128), F32)
                for s in range(SLOTS):
                    tile = s * CELLS + cell
                    r = radius[tile]
                    new = new_radius(r, sol[tile], wet)
                    alive = s < alive_count
                    rnew[tile] = jnp.where(alive, new * stays[tile], 0.0)
                    condensed = condensed + jnp.where(
                        alive, mult[tile] * (new * new * new - r * r * r), 0.0
                    )
                state[3, k, rows] = heat[0, cell] + (HEATING * UPTAKE) * condensed
                state[4, k, rows] = heat[1, cell] - UPTAKE * condensed

    staged(sums, cells)


def late_turn(
    chunk, codes, bin_of, table, values, places, picked, wet, supersat, radius, mult, sol, stays, out_acc
):
    table[...] = jnp.zeros_like(table)

    def spread_turn(t, _):
        tile = pl.ds(pl.multiple_of(t * 8, 8), 8)
        first = (chunk * BINS).astype(F32)
        bins8 = jnp.maximum(jnp.minimum(bin_of[tile] - first, float(BINS)), -1.0)
        lane8 = codes[3, tile]
        code8 = [codes[n, tile] for n in range(3)]
        hots = [to_bf16(iota((128, 128), 0).astype(F32) == lane8[q : q + 1]) for q in range(8)]
        spread = [spread_row(bins8[q : q + 1], code8, q) for q in range(8)]
        table[...] += dot(jnp.concatenate(spread, 1), jnp.concatenate(hots, 1), NT)
        return _

    lax.fori_loop(0, BLOCKS // 8, spread_turn, 0)
    groups, inners, places[0], places[1] = read_table(table)

    clear_left(groups, inners, stays, 1)
    gather(groups, inners, (radius, mult, sol), values, 1)
    grow_bins(groups, inners, supersat, wet, values, picked, 1)
    place_bins(
        lambda tile: [picked[tile], values[1, tile], values[2, tile]], places, out_acc, 1
    )


def local_kernel(
    pad, yhalo, radius, mult, sol, codes, bin_of, table, most, weights, values,
    picked, late, heat, supersat, stays,
    wet, lines, along, late_table, late_values, late_places, late_picked,
):
    chunks = (jnp.max(most[...]).astype(I32) + BINS - 1) // BINS
    late[...] = jnp.zeros_like(late)
    stays[...] = jnp.ones_like(stays)
    moisten(pad, yhalo, weights, heat, supersat, lines, along)
    groups, inners, _, _ = read_table(table)
    grow_bins(groups, inners, supersat, wet, values, picked, 8)

    def turn(chunk, _):
        late_turn(
            chunk, codes, bin_of, late_table, late_values, late_places, late_picked,
            wet, supersat, radius, mult, sol, stays, late,
        )
        return _

    lax.fori_loop(1, chunks, turn, 0)


def local_step(*operands):
    return pl.pallas_call(
        local_kernel,
        out_shape=(
            jax.ShapeDtypeStruct((BINS, 128), F32),
            jax.ShapeDtypeStruct((12 * HALF, 256), F32),
            jax.ShapeDtypeStruct((2, CELLS, 8, 128), F32),
            jax.ShapeDtypeStruct((CELLS, 8, 128), F32),
            jax.ShapeDtypeStruct((TILES, 8, 128), F32),
        ),
        in_specs=[VMEM_SPEC] * 11,
        out_specs=(VMEM_SPEC,) * 5,
        scratch_shapes=[
            pltpu.VMEM((1, BINS, 128), F32),
            pltpu.VMEM((4, 128, 512), BF16),
            pltpu.VMEM((4, 128, 384), F32),
            pltpu.VMEM((3 * BINS, 128), F32),
            pltpu.VMEM((3, BINS, 128), F32),
            pltpu.VMEM((2, BINS, 128), F32),
            pltpu.VMEM((BINS, 128), F32),
        ],
        compiler_params=pltpu.CompilerParams(vmem_limit_bytes=24 << 20),
    )(*operands)


def droplet_kernel(
    picked, values, places, table, late, pad, yhalo, radius, mult, sol, counts, stays, heat, supersat, weights,
    arrivals, state, rnew,
    out_acc, outgoing, lines, along, send_sem, recv_sem,
):
    east, west = ring("gx")
    north, south = ring("gy")
    ways = (east, west, north, south)
    greet(ways)
    out_acc[...] = late[...]
    place_bins(lambda tile: [picked[tile], values[1, tile], values[2, tile]], places, out_acc, PARTS)
    for d in range(4):
        for n in range(3):
            first = n * 2 * HALF + d * 8
            total = out_acc[first : first + 8] + out_acc[first + 6 * HALF : first + 6 * HALF + 8]
            outgoing[d, n, 0:8] = total[:, :128]
            outgoing[d, n, 8:16] = total[:, 128:]
    greeted(ways)
    sends = [
        pltpu.make_async_remote_copy(
            src_ref=outgoing.at[d],
            dst_ref=arrivals.at[:, d],
            send_sem=send_sem.at[d],
            recv_sem=recv_sem.at[d],
            device_id=there,
            device_id_type=MESH,
        )
        for d, there in enumerate(ways)
    ]
    for copy in sends:
        copy.start()
    finish(
        pad, yhalo, radius, mult, sol, counts, stays, heat, supersat, weights, state, rnew, lines, along
    )
    groups, inners, _, _ = read_table(table)
    clear_left(groups, inners, rnew, 8)
    for copy in sends:
        copy.wait()


def exchange_droplets(*operands):
    return pl.pallas_call(
        droplet_kernel,
        out_shape=(
            jax.ShapeDtypeStruct((3, 4, CAP // 128, 128), F32),
            jax.ShapeDtypeStruct((5, NZ, CX, CY), F32),
            jax.ShapeDtypeStruct((TILES, 8, 128), F32),
        ),
        in_specs=[VMEM_SPEC] * 15,
        out_specs=(ANY_SPEC, VMEM_SPEC, VMEM_SPEC),
        scratch_shapes=[
            pltpu.VMEM((12 * HALF, 256), F32),
            pltpu.VMEM((4, 3, CAP // 128, 128), F32),
            pltpu.VMEM((4, 192, 512), BF16),
            pltpu.VMEM((4, 192, 384), F32),
            pltpu.SemaphoreType.DMA((4,)),
            pltpu.SemaphoreType.DMA((4,)),
        ],
        compiler_params=pltpu.CompilerParams(
            collective_id=1, has_side_effects=True, vmem_limit_bytes=16 << 20
        ),
    )(*operands)


def store_kernel(*refs):
    *refs, sems = refs
    count = len(refs) // 2
    copies = [
        pltpu.make_async_copy(refs[n], refs[count + n], sems.at[n]) for n in range(count)
    ]
    for copy in copies:
        copy.start()
    for copy in copies:
        copy.wait()


def store(*arrays):
    return pl.pallas_call(
        store_kernel,
        out_shape=tuple(jax.ShapeDtypeStruct(a.shape, F32) for a in arrays),
        in_specs=[ANY_SPEC] * len(arrays),
        out_specs=(HBM_SPEC,) * len(arrays),
        scratch_shapes=[pltpu.SemaphoreType.DMA((len(arrays),))],
        compiler_params=pltpu.CompilerParams(vmem_limit_bytes=4 << 20),
    )(*arrays)


def per_device(
    velocity, theta_field, vapour, radius, multiplicity, solute, counts, leave_slot, leave_dir
):
    drops = (a.reshape(TILES, 8, 128) for a in (radius, multiplicity, solute))
    lists = (a.reshape(BLOCKS, 128) for a in (leave_slot, leave_dir))
    inputs = (velocity, theta_field, vapour, *drops, counts, *lists)
    *ready, values, places = exchange_halo(
        *(pltpu.with_memory_space_constraint(a, pltpu.HBM) for a in inputs)
    )
    pad, yhalo, radii, mult, sol, alive, codes, bin_of, table, most, weights = ready
    picked, late, heat, supersat, stays = local_step(
        pad, yhalo, radii, mult, sol, codes, bin_of, table, most, weights, values
    )
    arrivals, state_new, radius_new = store(
        *exchange_droplets(
            picked, values, places, table, late, pad, yhalo, radii, mult, sol, alive, stays, heat, supersat, weights
        )
    )
    return (state_new, radius_new.reshape(radius.shape), arrivals.reshape(3, 4, 1, 1, CAP))


def solution(mesh):
    in_specs = (
        P(None, None, "gx", "gy"),
        P(None, "gx", "gy"),
        P(None, "gx", "gy"),
        P(None, None, "gx", "gy"),
        P(None, None, "gx", "gy"),
        P(None, None, "gx", "gy"),
        P(None, "gx", "gy"),
        P("gx", "gy", None),
        P("gx", "gy", None),
    )
    out_specs = (
        P(None, None, "gx", "gy"),
        P(None, None, "gx", "gy"),
        P(None, None, "gx", "gy", None),
    )
    return jax.shard_map(
        per_device, mesh=mesh, in_specs=in_specs, out_specs=out_specs, check_vma=False
    )
```

```python
import functools

import jax
import jax.numpy as jnp
from jax import lax
from jax.experimental import pallas as pl
from jax.experimental.pallas import tpu as pltpu
from jax.sharding import PartitionSpec as P

MESH = pl.DeviceIdType.MESH
VMEM_SPEC = pl.BlockSpec(memory_space=pltpu.VMEM)
ANY_SPEC = pl.BlockSpec(memory_space=pl.ANY)
HBM_SPEC = pl.BlockSpec(memory_space=pltpu.HBM)

CX, CY, NZ, SLOTS, CAP, MIG = 16, 128, 16, 5, 2048, 8192
TILES = SLOTS * NZ * 2
CELLS = NZ * 2
BLOCKS = MIG // 128
BINS = 64
HALF = 16
GROUP = 6

TIME_STEP = 0.5
DIFFUSION = 0.05
BUOYANCY = 0.0327
SATURATION = 10.0
SAT_SLOPE = 0.06
GROWTH = 20.0
CURVATURE = 1.0
HYGROSCOPY = 1.0
FLOOR_SQUARE = 0.25
UPTAKE = 0.001
HEATING = 2.5

F32, BF16, I32 = jnp.float32, jnp.bfloat16, jnp.int32


def iota(shape, dim):
    return lax.broadcasted_iota(I32, shape, dim)


def ring(axis):
    count = lax.axis_size(axis)
    me = lax.axis_index(axis)
    return {axis: lax.rem(me + 1, count)}, {axis: lax.rem(me + count - 1, count)}


def greet(neighbours):
    for there in neighbours:
        pl.semaphore_signal(
            pltpu.get_barrier_semaphore(), inc=1, device_id=there, device_id_type=MESH
        )


def greeted(neighbours):
    pl.semaphore_wait(pltpu.get_barrier_semaphore(), len(neighbours))


def iota16(shape):
    return iota(shape, 0).astype(F32).astype(BF16)


def row16(tile, q, rows):
    return jnp.broadcast_to(tile[q : q + 1], (rows, 128)).astype(BF16)


def hot16(hit):
    return jnp.where(hit, jnp.ones(hit.shape, BF16), jnp.zeros(hit.shape, BF16))


def to_bf16(mask):
    return jnp.where(mask, 1.0, 0.0).astype(BF16)


NT = (((1,), (1,)), ((), ()))
NN = (((1,), (0,)), ((), ()))


def dot(a, b, dims=NN):
    return lax.dot_general(a, b, dims, preferred_element_type=F32)


def entry_codes(slots, ways, codes):
    before = iota((128, 128), 0) < iota((128, 128), 1)
    counter = jnp.concatenate([to_bf16(before), jnp.ones((128, 128), BF16)], 1)
    slot = slots[...]
    valid = slot >= 0
    way = jnp.where(valid, ways[...], -1)
    marks = [jnp.where(way == d, 1.0, 0.0) for d in range(4)]
    inside = dot(jnp.concatenate(marks, 0).astype(BF16), counter)
    earlier = to_bf16(iota((BLOCKS, BLOCKS), 1) < iota((BLOCKS, BLOCKS), 0))
    rank = jnp.zeros((BLOCKS, 128), F32)
    for d in range(4):
        block = inside[d * BLOCKS : (d + 1) * BLOCKS]
        offset = dot(earlier, block[:, 128:].astype(BF16))
        rank = rank + marks[d] * (block[:, :128] + offset)
    rank = rank.astype(I32)
    row = lax.shift_right_logical(slot, 7)
    inner = row & 7
    place_row = (way << 3) + (lax.shift_right_logical(rank, 7) & 7)
    column = (rank & 127) + (lax.shift_right_logical(rank, 10) << 7)
    codes[0] = jnp.where(valid, lax.shift_right_logical(row, 3) + 1, 0).astype(F32)
    codes[1] = column.astype(F32)
    codes[2] = (inner + (place_row << 3)).astype(F32)
    codes[3] = jnp.where(valid, slot & 127, -1).astype(F32)
    return counter


def spread_row(number, code8, q):
    hit = iota16((BINS, 128)) == jnp.broadcast_to(number, (BINS, 128)).astype(BF16)
    spread = []
    for n in range(3):
        value = row16(code8[n], q, BINS)
        spread.append(jnp.where(hit, value, jnp.zeros_like(value)))
    return jnp.concatenate(spread, 0)


def bin_lists(counter, codes, bin_of, table, most):
    table[...] = jnp.zeros_like(table)

    def turn(t, carry):
        tile = pl.ds(pl.multiple_of(t * 8, 8), 8)
        lane8 = codes[3, tile]
        code8 = [codes[n, tile] for n in range(3)]
        found, hots, spread = [], [], []
        for q in range(8):
            hit = iota((128, 128), 0).astype(F32) == lane8[q : q + 1]
            hots.append(to_bf16(hit))
            counted = dot(hots[-1], counter)
            number = jnp.sum(
                jnp.where(hit, counted[:, :128] + carry, 0.0), axis=0, keepdims=True
            )
            carry = carry + counted[:, 128:]
            found.append(number)
            spread.append(spread_row(jnp.minimum(number, float(BINS)), code8, q))
        bin_of[tile] = jnp.concatenate(found, 0)
        table[...] += dot(jnp.concatenate(spread, 1), jnp.concatenate(hots, 1), NT)
        return carry

    most[...] = lax.fori_loop(0, BLOCKS // 8, turn, jnp.zeros((128, 128), F32), unroll=8)


PARTS = BINS // 8


def read_table(table):
    first = table[0:BINS].astype(I32)
    third = table[2 * BINS : 3 * BINS].astype(I32)
    group = first - 1
    inner = third & 7
    groups = [group[8 * m : 8 * m + 8] for m in range(PARTS)]
    inners = [inner[8 * m : 8 * m + 8] for m in range(PARTS)]
    place_row = jnp.where(first > 0, lax.shift_right_logical(third, 3), -1).astype(F32)
    return groups, inners, place_row, table[BINS : 2 * BINS]


def gather(groups, inners, sources, values, unroll):
    count = len(sources)

    def turn(j, kept):
        tiles = [source[j] for source in sources]
        kept = list(kept)
        for m in range(PARTS):
            hit = groups[m] == j
            for n in range(count):
                got = jnp.take_along_axis(tiles[n], inners[m], axis=0, mode="promise_in_bounds")
                kept[n * PARTS + m] = jnp.where(hit, got, kept[n * PARTS + m])
        return tuple(kept)

    start = tuple(jnp.zeros((8, 128), F32) for _ in range(count * PARTS))
    kept = lax.fori_loop(0, sources[0].shape[0], turn, start, unroll=unroll)
    for n in range(count):
        for m in range(PARTS):
            values[n, 8 * m : 8 * m + 8] = kept[n * PARTS + m]


def clear_left(groups, inners, slots, unroll):
    bits = [jnp.left_shift(1, inners[m]) for m in range(PARTS)]
    sublane = iota((8, 128), 0)

    def turn(j, _):
        marked = jnp.zeros((8, 128), I32)
        for m in range(PARTS):
            marked = marked | jnp.where(groups[m] == j, bits[m], 0)
        marked = marked | pltpu.roll(marked, 4, 0)
        marked = marked | pltpu.roll(marked, 2, 0)
        marked = marked | pltpu.roll(marked, 1, 0)
        left = (lax.shift_right_logical(marked, sublane) & 1) == 1
        slots[j] = jnp.where(left, 0.0, slots[j])
        return _

    lax.fori_loop(0, TILES, turn, 0, unroll=unroll)


def new_radius(r, solute, supersat):
    inv = 1.0 / r
    square = r * r + GROWTH * (
        supersat - CURVATURE * inv + (HYGROSCOPY * solute) * (inv * inv * inv)
    )
    return jnp.sqrt(jnp.maximum(square, FLOOR_SQUARE))


def grow_bins(groups, inners, supersat, wet, values, picked, unroll):
    gather([group & (CELLS - 1) for group in groups], inners, (supersat,), wet, unroll)
    for m in range(PARTS):
        rows = slice(8 * m, 8 * m + 8)
        r = jnp.where(groups[m] < 0, 1.0, values[0, rows])
        picked[rows] = new_radius(r, values[2, rows], wet[0, rows])


def place_bins(tile_of, places, out_acc, unroll):
    def turn(t, _):
        tile = pl.ds(pl.multiple_of(t * 8, 8), 8)
        row8, column8 = places[0, tile], places[1, tile]
        whole = tile_of(tile)
        high = [value.astype(BF16).astype(F32) for value in whole]
        low = [value - part for value, part in zip(whole, high)]
        rows, columns = [], []
        for q in range(8):
            hit = iota16((2 * HALF, 128)) == row16(row8, q, 2 * HALF)
            parts = []
            for piece in high + low:
                value = row16(piece, q, 2 * HALF)
                parts.append(jnp.where(hit, value, jnp.zeros_like(value)))
            rows.append(jnp.concatenate(parts, 0))
            columns.append(hot16(iota16((256, 128)) == row16(column8, q, 256)))
        out_acc[...] += dot(jnp.concatenate(rows, 1), jnp.concatenate(columns, 1), NT)
        return _

    lax.fori_loop(0, PARTS, turn, 0, unroll=unroll)


def halo_kernel(
    vel, theta, vap, radius_in, mult_in, sol_in, counts_in, slots_in, ways_in,
    pad, yhalo, radius, mult, sol, counts, codes, bin_of, table, most, weights, values, places,
    packed, landed, slots, ways, local_sem, send_sem, recv_sem,
):
    east, west = ring("gx")
    north, south = ring("gy")
    neighbours = (east, west, north, south)
    greet(neighbours)
    pairs = (
        (slots_in, slots),
        (ways_in, ways),
        (vel, pad.at[0:3, :, 8:24, :]),
        (theta, pad.at[3, :, 8:24, :]),
        (vap, pad.at[4, :, 8:24, :]),
        (radius_in, radius),
        (mult_in, mult),
        (sol_in, sol),
        (counts_in, counts),
    )
    loads = [
        pltpu.make_async_copy(source, target, local_sem.at[number])
        for number, (source, target) in enumerate(pairs)
    ]
    for copy in loads:
        copy.start()
    weights[...] = line_weights()
    for copy in loads[2:5]:
        copy.wait()

    turned = lax.rem(iota((16, 128), 1) + 3, 128)
    number = turned // GROUP

    def pack(quarter, _):
        total = jnp.zeros((16, 128), F32)
        for inner_level in range(4):
            for f in range(5):
                g = inner_level * 5 + f
                value = pad[f, quarter * 4 + inner_level, 8:24]
                if g:
                    value = pltpu.roll(value, GROUP * g, 1)
                total = jnp.where(number == g, value, total)
        packed[quarter] = total
        return _

    routes = (
        (pad.at[0:3, :, 21:24, :], pad.at[0:3, :, 5:8, :], east),
        (pad.at[0:3, :, 8:11, :], pad.at[0:3, :, 24:27, :], west),
        (pad.at[3:5, :, 21:24, :], pad.at[3:5, :, 5:8, :], east),
        (pad.at[3:5, :, 8:11, :], pad.at[3:5, :, 24:27, :], west),
        (packed, landed.at[0], north),
        (packed, landed.at[1], south),
    )
    sends = [
        pltpu.make_async_remote_copy(
            src_ref=source,
            dst_ref=target,
            send_sem=send_sem.at[number],
            recv_sem=recv_sem.at[number],
            device_id=there,
            device_id_type=MESH,
        )
        for number, (source, target, there) in enumerate(routes)
    ]
    lax.fori_loop(0, 4, pack, 0, unroll=4)
    greeted(neighbours)
    for copy in sends:
        copy.start()
    for copy in loads[:2]:
        copy.wait()
    bin_lists(entry_codes(slots, ways, codes), codes, bin_of, table, most)
    for copy in loads[5:]:
        copy.wait()
    groups, inners, places[0], places[1] = read_table(table)
    gather(groups, inners, (radius, mult, sol), values, 8)
    sends[4].wait_recv()
    sends[5].wait_recv()
    from_south = turned - number * GROUP < 3
    for quarter in range(4):
        yhalo[quarter] = jnp.where(from_south, landed[0, quarter], landed[1, quarter])
    for copy in sends[:4]:
        copy.wait_recv()
    for copy in sends:
        copy.wait_send()


def exchange_halo(velocity, theta_field, vapour, radius, multiplicity, solute, counts, slots, ways):
    drops = jax.ShapeDtypeStruct((TILES, 8, 128), F32)
    return pl.pallas_call(
        halo_kernel,
        out_shape=(
            jax.ShapeDtypeStruct((5, NZ, 32, CY), F32),
            jax.ShapeDtypeStruct((4, 16, 128), F32),
            drops,
            drops,
            drops,
            jax.ShapeDtypeStruct((NZ, CX, CY), I32),
            jax.ShapeDtypeStruct((4, BLOCKS, 128), F32),
            jax.ShapeDtypeStruct((BLOCKS, 128), F32),
            jax.ShapeDtypeStruct((3 * BINS, 128), F32),
            jax.ShapeDtypeStruct((128, 128), F32),
            jax.ShapeDtypeStruct((512, 384), BF16),
            jax.ShapeDtypeStruct((3, BINS, 128), F32),
            jax.ShapeDtypeStruct((2, BINS, 128), F32),
        ),
        in_specs=[HBM_SPEC] * 9,
        out_specs=(VMEM_SPEC,) * 13,
        scratch_shapes=[
            pltpu.VMEM((4, 16, 128), F32),
            pltpu.VMEM((2, 4, 16, 128), F32),
            pltpu.VMEM((BLOCKS, 128), I32),
            pltpu.VMEM((BLOCKS, 128), I32),
            pltpu.SemaphoreType.DMA((9,)),
            pltpu.SemaphoreType.DMA((6,)),
            pltpu.SemaphoreType.DMA((6,)),
        ],
        compiler_params=pltpu.CompilerParams(
            collective_id=0, has_side_effects=True, vmem_limit_bytes=24 << 20
        ),
    )(velocity, theta_field, vapour, radius, multiplicity, solute, counts, slots, ways)


def line_weights():
    apart = iota((128, 128), 0) - iota((128, 128), 1)

    def weights(far):
        size = jnp.abs(far)
        sign = jnp.where(far < 0, -1.0, 1.0)
        centred = jnp.where(size == 1, 45.0, jnp.where(size == 2, -9.0, jnp.where(size == 3, 1.0, 0.0)))
        damping = jnp.where(
            size == 0, -20.0,
            jnp.where(size == 1, 15.0, jnp.where(size == 2, -6.0, jnp.where(size == 3, 1.0, 0.0))),
        )
        beside = jnp.where(size == 1, 1.0, 0.0)
        return jnp.concatenate([centred * sign, damping, beside], 1)

    own = weights(apart)
    halo = weights(apart + 128) + weights(apart - 128)
    return jnp.concatenate([own, own, halo, halo], 0).astype(BF16)


def line_sums(quarter, fields, pad, yhalo, weights, lines, along):
    for inner_level in range(4):
        for position, f in enumerate(fields):
            g = inner_level * 5 + f
            edge = yhalo[quarter]
            if g:
                edge = pltpu.roll(edge, 128 - GROUP * g, 1)
            first = 16 * (inner_level * len(fields) + position)
            for part, value in enumerate((pad[f, quarter * 4 + inner_level, 8:24], edge)):
                high = value.astype(BF16)
                low = (value - high.astype(F32)).astype(BF16)
                lines[quarter, first : first + 16, 256 * part : 256 * part + 128] = high
                lines[quarter, first : first + 16, 256 * part + 128 : 256 * part + 256] = low
    along[quarter] = dot(lines[quarter], weights[...])


def advance(quarter, inner_level, half, fields, pad, along):
    k = quarter * 4 + inner_level
    above, below = min(k + 1, NZ - 1), max(k - 1, 0)
    base = 8 + 8 * half
    u = pad[0, k, base : base + 8] * (-TIME_STEP / 60.0)
    v = pad[1, k, base : base + 8] * (-TIME_STEP / 60.0)
    w = pad[2, k, base : base + 8]
    lift = DIFFUSION * TIME_STEP - w * (0.5 * TIME_STEP)
    sink = DIFFUSION * TIME_STEP + w * (0.5 * TIME_STEP)
    u_size, v_size = jnp.abs(u), jnp.abs(v)
    moved = []
    for position, f in enumerate(fields):
        mid = pad[f, k, base : base + 8]
        p1, m1, p2, m2, p3, m3 = (
            pad[f, k, base + d : base + d + 8] for d in (1, -1, 2, -2, 3, -3)
        )
        first = 16 * (inner_level * len(fields) + position) + 8 * half
        y_centred, y_damping, y_beside = (
            along[quarter, first : first + 8, 128 * n : 128 * n + 128] for n in range(3)
        )
        s1 = p1 + m1
        total = mid + u * (45.0 * (p1 - m1) - 9.0 * (p2 - m2) + (p3 - m3))
        total = total + u_size * (15.0 * s1 - 6.0 * (p2 + m2) + (p3 + m3) - 20.0 * mid)
        total = total + v * y_centred + v_size * y_damping
        total = total + (DIFFUSION * TIME_STEP) * (s1 + y_beside - 6.0 * mid)
        total = total + lift * pad[f, above, base : base + 8] + sink * pad[f, below, base : base + 8]
        if f == 2:
            total = total + (TIME_STEP * BUOYANCY) * pad[3, k, base : base + 8]
        moved.append(total)
    return moved


def staged(first_step, second_step):
    first_step(0)
    for quarter in range(4):
        if quarter < 3:
            first_step(quarter + 1)
        second_step(quarter)


def moisten(pad, yhalo, weights, heat, supersat, lines, along):
    fields = (3, 4)

    def sums(quarter):
        line_sums(quarter, fields, pad, yhalo, weights, lines, along)

    def cells(quarter):
        for inner_level in range(4):
            for half in range(2):
                tile = (quarter * 4 + inner_level) * 2 + half
                theta, vapour = advance(quarter, inner_level, half, fields, pad, along)
                heat[0, tile] = theta
                heat[1, tile] = vapour
                supersat[tile] = vapour * (jnp.exp(-SAT_SLOPE * theta) * (1.0 / SATURATION)) - 1.0

    staged(sums, cells)


def finish(
    pad, yhalo, radius, mult, sol, counts, stays, heat, supersat, weights, state, rnew, lines, along
):
    fields = (0, 1, 2)

    def sums(quarter):
        line_sums(quarter, fields, pad, yhalo, weights, lines, along)

    def cells(quarter):
        for inner_level in range(4):
            k = quarter * 4 + inner_level
            for half in range(2):
                rows = slice(8 * half, 8 * half + 8)
                cell = k * 2 + half
                for f, value in enumerate(advance(quarter, inner_level, half, fields, pad, along)):
                    state[f, k, rows] = value
                alive_count, wet = counts[k, rows], supersat[cell]
                condensed = jnp.zeros((8, 128), F32)
                for s in range(SLOTS):
                    tile = s * CELLS + cell
                    r = radius[tile]
                    new = new_radius(r, sol[tile], wet)
                    alive = s < alive_count
                    rnew[tile] = jnp.where(alive, new * stays[tile], 0.0)
                    condensed = condensed + jnp.where(
                        alive, mult[tile] * (new * new * new - r * r * r), 0.0
                    )
                state[3, k, rows] = heat[0, cell] + (HEATING * UPTAKE) * condensed
                state[4, k, rows] = heat[1, cell] - UPTAKE * condensed

    staged(sums, cells)


def late_turn(
    chunk, codes, bin_of, table, values, places, picked, wet, supersat, radius, mult, sol, stays, out_acc
):
    table[...] = jnp.zeros_like(table)

    def spread_turn(t, _):
        tile = pl.ds(pl.multiple_of(t * 8, 8), 8)
        first = (chunk * BINS).astype(F32)
        bins8 = jnp.maximum(jnp.minimum(bin_of[tile] - first, float(BINS)), -1.0)
        lane8 = codes[3, tile]
        code8 = [codes[n, tile] for n in range(3)]
        hots = [to_bf16(iota((128, 128), 0).astype(F32) == lane8[q : q + 1]) for q in range(8)]
        spread = [spread_row(bins8[q : q + 1], code8, q) for q in range(8)]
        table[...] += dot(jnp.concatenate(spread, 1), jnp.concatenate(hots, 1), NT)
        return _

    lax.fori_loop(0, BLOCKS // 8, spread_turn, 0)
    groups, inners, places[0], places[1] = read_table(table)

    clear_left(groups, inners, stays, 1)
    gather(groups, inners, (radius, mult, sol), values, 1)
    grow_bins(groups, inners, supersat, wet, values, picked, 1)
    place_bins(
        lambda tile: [picked[tile], values[1, tile], values[2, tile]], places, out_acc, 1
    )


def local_kernel(
    pad, yhalo, radius, mult, sol, codes, bin_of, table, most, weights, values,
    picked, late, heat, supersat, stays,
    wet, lines, along, late_table, late_values, late_places, late_picked,
):
    chunks = (jnp.max(most[...]).astype(I32) + BINS - 1) // BINS
    late[...] = jnp.zeros_like(late)
    stays[...] = jnp.ones_like(stays)
    moisten(pad, yhalo, weights, heat, supersat, lines, along)
    groups, inners, _, _ = read_table(table)
    grow_bins(groups, inners, supersat, wet, values, picked, 8)

    def turn(chunk, _):
        late_turn(
            chunk, codes, bin_of, late_table, late_values, late_places, late_picked,
            wet, supersat, radius, mult, sol, stays, late,
        )
        return _

    lax.fori_loop(1, chunks, turn, 0)


def local_step(*operands):
    return pl.pallas_call(
        local_kernel,
        out_shape=(
            jax.ShapeDtypeStruct((BINS, 128), F32),
            jax.ShapeDtypeStruct((12 * HALF, 256), F32),
            jax.ShapeDtypeStruct((2, CELLS, 8, 128), F32),
            jax.ShapeDtypeStruct((CELLS, 8, 128), F32),
            jax.ShapeDtypeStruct((TILES, 8, 128), F32),
        ),
        in_specs=[VMEM_SPEC] * 11,
        out_specs=(VMEM_SPEC,) * 5,
        scratch_shapes=[
            pltpu.VMEM((1, BINS, 128), F32),
            pltpu.VMEM((4, 128, 512), BF16),
            pltpu.VMEM((4, 128, 384), F32),
            pltpu.VMEM((3 * BINS, 128), F32),
            pltpu.VMEM((3, BINS, 128), F32),
            pltpu.VMEM((2, BINS, 128), F32),
            pltpu.VMEM((BINS, 128), F32),
        ],
        compiler_params=pltpu.CompilerParams(vmem_limit_bytes=24 << 20),
    )(*operands)


def droplet_kernel(
    picked, values, places, table, late, pad, yhalo, radius, mult, sol, counts, stays, heat, supersat, weights,
    arrivals, state, rnew,
    out_acc, outgoing, lines, along, send_sem, recv_sem,
):
    east, west = ring("gx")
    north, south = ring("gy")
    ways = (east, west, north, south)
    greet(ways)
    out_acc[...] = late[...]
    place_bins(lambda tile: [picked[tile], values[1, tile], values[2, tile]], places, out_acc, PARTS)
    for d in range(4):
        for n in range(3):
            first = n * 2 * HALF + d * 8
            total = out_acc[first : first + 8] + out_acc[first + 6 * HALF : first + 6 * HALF + 8]
            outgoing[d, n, 0:8] = total[:, :128]
            outgoing[d, n, 8:16] = total[:, 128:]
    greeted(ways)
    sends = [
        pltpu.make_async_remote_copy(
            src_ref=outgoing.at[d],
            dst_ref=arrivals.at[:, d],
            send_sem=send_sem.at[d],
            recv_sem=recv_sem.at[d],
            device_id=there,
            device_id_type=MESH,
        )
        for d, there in enumerate(ways)
    ]
    for copy in sends:
        copy.start()
    finish(
        pad, yhalo, radius, mult, sol, counts, stays, heat, supersat, weights, state, rnew, lines, along
    )
    groups, inners, _, _ = read_table(table)
    clear_left(groups, inners, rnew, 8)
    for copy in sends:
        copy.wait()


def exchange_droplets(*operands):
    return pl.pallas_call(
        droplet_kernel,
        out_shape=(
            jax.ShapeDtypeStruct((3, 4, CAP // 128, 128), F32),
            jax.ShapeDtypeStruct((5, NZ, CX, CY), F32),
            jax.ShapeDtypeStruct((TILES, 8, 128), F32),
        ),
        in_specs=[VMEM_SPEC] * 15,
        out_specs=(ANY_SPEC, VMEM_SPEC, VMEM_SPEC),
        scratch_shapes=[
            pltpu.VMEM((12 * HALF, 256), F32),
            pltpu.VMEM((4, 3, CAP // 128, 128), F32),
            pltpu.VMEM((4, 192, 512), BF16),
            pltpu.VMEM((4, 192, 384), F32),
            pltpu.SemaphoreType.DMA((4,)),
            pltpu.SemaphoreType.DMA((4,)),
        ],
        compiler_params=pltpu.CompilerParams(
            collective_id=1, has_side_effects=True, vmem_limit_bytes=16 << 20
        ),
    )(*operands)


def store_kernel(*refs):
    *refs, sems = refs
    count = len(refs) // 2
    copies = []
    for n in range(count):
        size = refs[n].shape[0]
        step = -(-size // 5)
        for first in range(0, size, step):
            rows = slice(first, min(first + step, size))
            copies.append(
                pltpu.make_async_copy(
                    refs[n].at[rows], refs[count + n].at[rows], sems.at[len(copies)]
                )
            )
    for copy in copies:
        copy.start()
    for copy in copies:
        copy.wait()


def store(*arrays):
    return pl.pallas_call(
        store_kernel,
        out_shape=tuple(jax.ShapeDtypeStruct(a.shape, F32) for a in arrays),
        in_specs=[ANY_SPEC] * len(arrays),
        out_specs=(HBM_SPEC,) * len(arrays),
        scratch_shapes=[pltpu.SemaphoreType.DMA((5 * len(arrays),))],
        compiler_params=pltpu.CompilerParams(vmem_limit_bytes=4 << 20),
    )(*arrays)


def per_device(
    velocity, theta_field, vapour, radius, multiplicity, solute, counts, leave_slot, leave_dir
):
    drops = (a.reshape(TILES, 8, 128) for a in (radius, multiplicity, solute))
    lists = (a.reshape(BLOCKS, 128) for a in (leave_slot, leave_dir))
    inputs = (velocity, theta_field, vapour, *drops, counts, *lists)
    *ready, values, places = exchange_halo(
        *(pltpu.with_memory_space_constraint(a, pltpu.HBM) for a in inputs)
    )
    pad, yhalo, radii, mult, sol, alive, codes, bin_of, table, most, weights = ready
    picked, late, heat, supersat, stays = local_step(
        pad, yhalo, radii, mult, sol, codes, bin_of, table, most, weights, values
    )
    arrivals, state_new, radius_new = store(
        *exchange_droplets(
            picked, values, places, table, late, pad, yhalo, radii, mult, sol, alive, stays, heat, supersat, weights
        )
    )
    return (state_new, radius_new.reshape(radius.shape), arrivals.reshape(3, 4, 1, 1, CAP))


def solution(mesh):
    in_specs = (
        P(None, None, "gx", "gy"),
        P(None, "gx", "gy"),
        P(None, "gx", "gy"),
        P(None, None, "gx", "gy"),
        P(None, None, "gx", "gy"),
        P(None, None, "gx", "gy"),
        P(None, "gx", "gy"),
        P("gx", "gy", None),
        P("gx", "gy", None),
    )
    out_specs = (
        P(None, None, "gx", "gy"),
        P(None, None, "gx", "gy"),
        P(None, None, "gx", "gy", None),
    )
    return jax.shard_map(
        per_device, mesh=mesh, in_specs=in_specs, out_specs=out_specs, check_vma=False
    )
```
